32 devices in a mesh: grp: 4 (over z), pb: 8 (over y, x, core).
Axes of the slice: x: 2, y: 2, z: 4, core: 2. Of those that a mesh axis runs over, the one named last changes fastest.
Arguments:
- queries: bfloat16 [2048, 4096], P('grp', 'pb'), may hold values from -12 to 12
- outputs: bfloat16 [2048, 4096], P('grp', 'pb'), may hold values from -3 to 3
- readout_grad: bfloat16 [2048, 8192], P('grp', 'pb'), may hold values from -24 to 24
- readout_weight: bfloat16 [4096, 8192], P('pb'), may hold values from -0.09375 to 0.09375
- log_norm: float32 [2048, 32], P('grp', 'pb'), may hold values from 9 to 11
- probes: int32 [32, 2048, 4], P('pb', 'grp'), may hold values from 0 to 31, all different within a row; in each aligned block of 512 rows (0 to 511, 512 to 1023, ..., all dimensions but the last counted through in order) at most 128 rows name the same one
- owner_slots: int32 [32, 32], P('pb'), may hold values from 0 to 31, each once within a row
- counts: int32 [32, 32], P('pb', 'grp'), may hold values from 1 to 512
- cluster_keys: bfloat16 [32, 32, 512, 128], P('pb', 'grp'), may hold values from -6 to 6
- values: bfloat16 [32, 32, 512, 128], P('pb', 'grp'), may hold values from -6 to 6
Outputs:
- query_grad: bfloat16 [2048, 4096], P('grp', 'pb')
The draws below stay inside these ranges and needn't reach their ends.
Inputs may be any that keep to these rules, and one draw needn't show every extreme that they name: `probes`: each token names 4 different clusters for each head. Within the 512 tokens of one index of grp and one head, no cluster is named by more than 128 tokens, a bound that some block reaches. `owner_slots`: for each head a permutation of the 32 clusters; slot s is stored on index s // 8 of grp.
All inputs are finite; a program needn't handle non-finite values.
Results may differ from the reference program's by a relative error of at most 0.029.
Values may be sent and summed in bfloat16 or wider, within the bound.
A program may use at most 128 MiB of HBM per device.

```python
import math
import jax
import jax.numpy as jnp
import numpy as np
from jax import lax

D = 8192
H = 32
DH = 128
S = 512
PROBES = 4
TOK_GRP = 512
NCL = 32
MOST = 128
TOKENS = 2048
N_GRP = 4


def touch_ends(result, key, smallest, largest):
    extent = result.shape
    spot = [jax.random.randint(jax.random.fold_in(key, axis), (), 0, extent[axis]) for axis in range(len(extent))]
    result = result.at[tuple(spot)].set(smallest)
    longest = extent.index(max(extent))
    spot[longest] = (spot[longest] + 1) % extent[longest]
    return result.at[tuple(spot)].set(largest)


def with_spikes(result, key, source, target, blocks, factor):
    owner, partner = [(jnp.arange(result.shape[dim]) // (result.shape[dim] // blocks)).reshape([-1 if axis == dim else 1 for axis in range(result.ndim)]) for dim in (source, target)]
    chosen = jax.random.permutation(key, blocks)[partner]
    strong = (owner == chosen) | (owner == (partner + blocks // 2) % blocks)
    return jnp.where(strong, factor * result, result)


def shard_levels(own_key, extent, cuts, smallest, largest):
    def one(dim, shards_of):
        steps = jax.random.uniform(jax.random.fold_in(jax.random.fold_in(own_key, 6), dim), (shards_of,), jnp.float32, smallest / len(cuts), largest / len(cuts))
        return jnp.repeat(jnp.exp(steps), extent[dim] // shards_of).reshape((-1,) + (1,) * (len(extent) - dim - 1))

    level = one(*cuts[0])
    for cut in cuts[1:]:
        level = level * one(*cut)
    return level


def assign_block(own_key, own, number, rows, count, top, limit, lean):
    order = jax.random.permutation(own_key, count)
    crowded, ordinary = shares(count, rows * top, limit, lean, True), shares(count, rows * top, limit, lean, False)
    places = jnp.arange(count)

    def named(lengths, turn):
        used = int((lengths > 0).sum())
        fixed = max(1, used // 4)
        shifted = fixed + (places - fixed + turn * (used - fixed)) % max(1, count - fixed)
        return jnp.zeros((count,), jnp.int32).at[order[jnp.where(places < fixed, places, shifted)]].set(jnp.asarray(lengths, jnp.int32))

    lengths = jnp.where(number % 4 == 0, named(crowded, number // 4), named(ordinary, number - number // 4 - 1))
    mixed = jax.random.permutation(jax.random.fold_in(own, 3), count)
    giver, taker = mixed[0:count // 2 * 2:2], mixed[1:count // 2 * 2:2]
    slack = jnp.minimum(lengths[giver] - 1, limit - lengths[taker]) // 2
    slack = jnp.where((giver == order[0]) | (taker == order[0]) | (lengths[taker] == 0), 0, jnp.maximum(slack, 0))
    shifted = jax.random.randint(jax.random.fold_in(own, 4), (count // 2,), 0, 1 << 20) % (slack + 1)
    lengths = lengths.at[giver].add(-shifted).at[taker].add(shifted)
    members = jnp.searchsorted(jnp.cumsum(lengths), jnp.arange(rows * top), side="right").astype(jnp.int32)
    listing = members.reshape(top, rows).T
    listing = listing[jax.random.permutation(jax.random.fold_in(own, 1), rows)]
    turn = jax.random.randint(jax.random.fold_in(own, 2), (rows, 1), 0, top)
    return jnp.take_along_axis(listing, (jnp.arange(top)[None, :] + turn) % top, axis=1)


def shares(number_of, total, reach, slope, full):
    weights = [(1 << 20) // math.isqrt(grade ** slope) + 1 for grade in range(1, number_of + 1)]
    largest = reach if full else min(reach, max(-(-total // number_of), total * weights[0] // sum(weights)))
    least = 1 if total - largest >= number_of - 1 else 0
    given, spare = [largest] + [least] * (number_of - 1), total - largest - least * (number_of - 1)
    while spare > 0:
        movable = [i for i in range(1, number_of) if given[i] < largest] or [i for i in range(1, number_of) if given[i] < reach]
        pool, left = sum([weights[i] for i in movable]), spare
        for i in movable:
            addition = min(reach - given[i], max(1, left * weights[i] // pool), spare)
            given[i] = given[i] + addition
            spare = spare - addition
    return np.array(given)


def scatter_about(stream_key, shape, deviation, limit, cuts=(), kind=jnp.bfloat16):
    array = jax.random.normal(stream_key, shape, jnp.float32) * deviation
    if len(cuts) > 0:
        array = shard_levels(stream_key, shape, cuts, -0.22, 0.18) * array
    return jnp.clip(array, min=-limit, max=limit).astype(kind)


def heavy_noise(own_key, dims, width, most, cuts, heavy, kind=jnp.bfloat16):
    values = width * jax.random.normal(own_key, dims, jnp.float32)
    if cuts:
        values = values * shard_levels(own_key, dims, cuts, -0.22, 0.18)
    return jnp.clip(with_spikes(values, jax.random.fold_in(own_key, 3), *heavy), -most, most).astype(kind)


def setup_inputs(seed: int = 0) -> dict:
    seeds = jax.random.split(jax.random.key(seed), 11)
    queries = scatter_about(seeds[0], (TOKENS, H * DH), 2.0, 12.0, ((0, 4), (1, 8)))
    outputs = scatter_about(seeds[1], (TOKENS, H * DH), 0.5, 3.0, ((0, 4), (1, 8)))
    readout_grad = scatter_about(seeds[2], (TOKENS, D), 4.0, 24.0, ((0, 4), (1, 8)))
    readout_weight = heavy_noise(seeds[3], (H * DH, D), D ** -0.5, 0.09375, ((0, 8),), (1, 0, 8, 2.0))
    log_norm = jnp.clip(9.0 + 2.0 * jax.random.uniform(seeds[4], (TOKENS, H), jnp.float32) ** shard_levels(seeds[4], (TOKENS, H), ((0, 4), (1, 8)), -0.2, 0.2), 9.0, 11.0)
    probes_keys = jax.random.split(jax.random.fold_in(seeds[5], 1), H * TOKENS // TOK_GRP)
    probes_turns = jax.random.permutation(jax.random.fold_in(seeds[5], 3), H * TOKENS // TOK_GRP)
    probes = jax.vmap(lambda own, number: assign_block(jax.random.fold_in(seeds[5], 2), own, number, TOK_GRP, NCL, PROBES, MOST, 2))(probes_keys, probes_turns).reshape((H, TOKENS, PROBES))
    owner_slots = jax.vmap(lambda own: jax.random.permutation(own, NCL))(jax.random.split(seeds[6], H)).reshape((H, NCL)).astype(jnp.int32)
    counts = touch_ends(jax.random.randint(seeds[7], (H, NCL), 1, S + 1), jax.random.fold_in(seeds[7], 1), 1, S).astype(jnp.int32)
    cluster_keys = scatter_about(seeds[8], (H, NCL, S, DH), 1.0, 6.0, ((0, 8), (1, 4)))
    values = scatter_about(seeds[9], (H, NCL, S, DH), 1.0, 6.0, ((0, 8), (1, 4)))
    return dict(queries=queries, outputs=outputs, readout_grad=readout_grad, readout_weight=readout_weight, log_norm=log_norm, probes=probes, owner_slots=owner_slots, counts=counts, cluster_keys=cluster_keys, values=values)


def head_places(probe_ids, slot_table):
    slot_ids = slot_table[probe_ids].astype(jnp.int32)
    blocked = slot_ids.reshape(N_GRP, TOK_GRP, PROBES)
    cluster_ids = jnp.arange(NCL, dtype=jnp.int32)
    marked = lax.optimization_barrier(jnp.sum((blocked[..., None] == cluster_ids).astype(jnp.int32), axis=2, dtype=jnp.int32))
    before = jnp.cumsum(marked, axis=1, dtype=jnp.int32) - marked
    ranking = jnp.take_along_axis(before, blocked, axis=2).astype(jnp.int32)
    group_ids = jnp.arange(N_GRP, dtype=jnp.int32)[:, None, None]
    places = blocked * (N_GRP * MOST) + group_ids * MOST + ranking
    return places.reshape(TOKENS * PROBES).astype(jnp.int32)

def block_grad(pieces):
    query_block, grad_block, norm_block, delta_block, key_block, value_block, valid = pieces
    score_scale = DH ** (-0.5)
    scores = jnp.dot(query_block, key_block.T, preferred_element_type=jnp.float32) * score_scale
    valid_keys = jnp.arange(S, dtype=jnp.int32)[None, :] < valid
    weights = jnp.where(valid_keys, jnp.exp(scores - norm_block[:, None]), jnp.zeros_like(scores))
    grad_prob = jnp.dot(grad_block, value_block.T, preferred_element_type=jnp.float32)
    grad_score = (weights * (grad_prob - delta_block[:, None])).astype(jnp.bfloat16)
    return (jnp.dot(grad_score, key_block, preferred_element_type=jnp.float32) * score_scale).astype(jnp.bfloat16)

def reference(queries, outputs, readout_grad, readout_weight, log_norm, probes, owner_slots, counts, cluster_keys, values):
    grad_out = jnp.dot(readout_grad, readout_weight.T, preferred_element_type=jnp.float32).astype(jnp.bfloat16)
    row_delta = lax.optimization_barrier(jnp.sum((grad_out.astype(jnp.float32) * outputs.astype(jnp.float32)).reshape(TOKENS, H, DH), axis=2))
    query_heads = queries.reshape(TOKENS, H, DH).transpose(1, 0, 2)
    grad_heads = grad_out.reshape(TOKENS, H, DH).transpose(1, 0, 2)
    arrivals = N_GRP * MOST
    slot_total = NCL * arrivals

    def one_head(pieces):
        query_head, grad_head, norm_head, delta_head, probe_head, table_head, count_head, key_head, value_head = pieces
        places = head_places(probe_head, table_head)

        def spread(rows):
            repeated = jnp.repeat(rows, PROBES, axis=0)
            blank_rows = jnp.zeros((slot_total,) + rows.shape[1:], rows.dtype)
            return blank_rows.at[places].set(repeated).reshape((NCL, arrivals) + rows.shape[1:])
        partials = lax.map(block_grad, (spread(query_head), spread(grad_head), spread(norm_head), spread(delta_head), key_head, value_head, count_head))
        picked = partials.reshape(slot_total, DH)[places].reshape(TOKENS, PROBES, DH)
        return lax.optimization_barrier(jnp.sum(picked.astype(jnp.float32), axis=1)).astype(jnp.bfloat16)
    grads = lax.map(one_head, (query_heads, grad_heads, log_norm.T, row_delta.T, probes, owner_slots, counts, cluster_keys, values))
    return grads.transpose(1, 0, 2).reshape(TOKENS, H * DH)
```

```python
import functools

import jax
import jax.numpy as jnp
from jax import lax
from jax.experimental import pallas as pl
from jax.experimental.pallas import tpu as pltpu
from jax.sharding import PartitionSpec as P

LANES = 128
AUX = 8
PAIR = 2


def three_parts(x):
    high = lax.reduce_precision(x, 8, 7)
    rest = x - high
    middle = lax.reduce_precision(rest, 8, 7)
    return jnp.stack([high, middle, rest - middle], axis=-1)


def probe_ranks(probes, owner_slots, local_clusters, token_count, groups):
    me = lax.axis_index("grp")
    clusters = owner_slots.shape[1]
    cluster_ids = jnp.arange(clusters, dtype=jnp.int32)
    slots = me * local_clusters + jnp.arange(local_clusters, dtype=jnp.int32)
    named = jnp.sum(
        jnp.where(owner_slots[:, None, :] == slots[None, :, None], cluster_ids, 0), axis=2, dtype=jnp.int32
    )
    marked = jnp.any(probes[:, None, :, :] == named[:, :, None, None], axis=3)
    marked = marked.reshape(probes.shape[0], local_clusters, groups, token_count)
    earlier = jnp.arange(token_count)[:, None] < jnp.arange(token_count)[None, :]
    before = lax.dot_general(
        marked.astype(jnp.bfloat16),
        earlier.astype(jnp.bfloat16),
        (((3,), (0,)), ((), ())),
        preferred_element_type=jnp.float32,
    )
    return jnp.where(marked, before.astype(jnp.int32), -1)


def grad_kernel(groups, capacity, scale, counts, q, g, aux, rows, cols, keys, values, out, total):
    head, step = pl.program_id(0), pl.program_id(1)
    token_count = q.shape[0] // groups
    span = keys.shape[2]
    lane = lax.broadcasted_iota(jnp.int32, (span, LANES), 1)
    key_id = lax.broadcasted_iota(jnp.int32, (span, LANES), 0)
    own = lane - head * AUX
    ones = jnp.where((own >= 0) & (own < 3), 1.0, 0.0)
    value_side = jnp.where((own >= 3) & (own < 6), 1.0, 0.0).astype(jnp.bfloat16)
    place = lax.broadcasted_iota(jnp.int32, (capacity, token_count), 0)
    contract_last = (((1,), (1,)), ((), ()))
    partials = []
    for i in range(PAIR):
        valid = counts[head, step * PAIR + i]
        key_side = jnp.where((lane == LANES - 1) & (key_id >= valid), -1e30, ones).astype(jnp.bfloat16)
        key_block, value_block = keys[0, i], values[0, i]
        picked = []
        for group in range(groups):
            span_of = pl.ds(group * token_count, token_count)
            chosen = (rows[0, i, :, span_of] == place).astype(jnp.bfloat16)
            rhs = jnp.concatenate([q[span_of, :], aux[span_of, :], g[span_of, :]], axis=1)
            picked.append(jnp.dot(chosen, rhs, preferred_element_type=jnp.float32).astype(jnp.bfloat16))
        picked = jnp.concatenate(picked, axis=0)
        scores = lax.dot_general(
            picked[:, : 2 * LANES],
            jnp.concatenate([key_block, key_side], axis=1),
            contract_last,
            preferred_element_type=jnp.float32,
        )
        grad_prob = lax.dot_general(
            picked[:, LANES:],
            jnp.concatenate([value_side, value_block], axis=1),
            contract_last,
            preferred_element_type=jnp.float32,
        )
        grad_score = (jnp.exp(scores * scale) * grad_prob).astype(jnp.bfloat16)
        partials.append(jnp.dot(grad_score, key_block, preferred_element_type=jnp.float32).astype(jnp.bfloat16))
    spot = lax.broadcasted_iota(jnp.int32, (token_count, capacity), 1)
    for group in range(groups):
        span_of = pl.ds(group * token_count, token_count)
        chosen = jnp.concatenate(
            [(cols[0, 0, span_of, i : i + 1] == spot).astype(jnp.bfloat16) for i in range(PAIR)], axis=1
        )
        part = jnp.concatenate([p[group * capacity : (group + 1) * capacity] for p in partials], axis=0)
        add = jnp.dot(chosen, part, preferred_element_type=jnp.float32)

        @pl.when(step == 0)
        def _():
            total[span_of, :] = add

        @pl.when(step > 0)
        def _():
            total[span_of, :] += add

    @pl.when(step == pl.num_programs(1) - 1)
    def _():
        out[...] = (total[...] * scale).astype(out.dtype)


def shards(
    queries, outputs, readout_grad, readout_weight, log_norm, probes, owner_slots, counts, cluster_keys, values
):
    token_count = queries.shape[0]
    heads, local_clusters, span, width = cluster_keys.shape
    clusters = owner_slots.shape[1]
    groups = lax.axis_size("grp")
    capacity = 2 * token_count * probes.shape[2] // clusters
    scale = width ** (-0.5)
    every = groups * token_count

    all_probes = lax.all_gather(probes, "grp", axis=1, tiled=True)
    all_queries = lax.all_gather(queries, "grp", axis=0, tiled=True)
    ranks = probe_ranks(all_probes, owner_slots, local_clusters, token_count, groups)
    ranks = ranks.reshape(heads, local_clusters, 1, every)
    steps = local_clusters // PAIR
    rank_cols = ranks.reshape(heads, steps, PAIR, every).transpose(0, 1, 3, 2)

    grad_out = lax.dot_general(
        lax.all_gather(readout_grad, "pb", axis=1, tiled=True),
        readout_weight,
        (((1,), (1,)), ((), ())),
        preferred_element_type=jnp.float32,
    ).astype(jnp.bfloat16)
    row_delta = jnp.sum(
        (grad_out.astype(jnp.float32) * outputs.astype(jnp.float32)).reshape(token_count, heads, width), axis=2
    )
    aux = jnp.concatenate(
        [three_parts(log_norm * (-1.0 / scale)), three_parts(-row_delta), jnp.zeros((token_count, heads, 2))], axis=2
    ).reshape(token_count, heads * AUX)
    aux = jnp.concatenate(
        [aux, jnp.zeros((token_count, LANES - 1 - heads * AUX)), jnp.ones((token_count, 1))], axis=1
    ).astype(jnp.bfloat16)
    all_grads = lax.all_gather(jnp.concatenate([grad_out, aux], axis=1), "grp", axis=0, tiled=True)

    partial = pl.pallas_call(
        functools.partial(grad_kernel, groups, capacity, scale),
        grid=(heads, steps),
        in_specs=[
            pl.BlockSpec(memory_space=pltpu.SMEM),
            pl.BlockSpec((every, width), lambda h, c: (0, h)),
            pl.BlockSpec((every, width), lambda h, c: (0, h)),
            pl.BlockSpec((every, LANES), lambda h, c: (0, heads)),
            pl.BlockSpec((1, PAIR, 1, every), lambda h, c: (h, c, 0, 0)),
            pl.BlockSpec((1, 1, every, PAIR), lambda h, c: (h, c, 0, 0)),
            pl.BlockSpec((1, PAIR, span, width), lambda h, c: (h, c, 0, 0)),
            pl.BlockSpec((1, PAIR, span, width), lambda h, c: (h, c, 0, 0)),
        ],
        out_specs=pl.BlockSpec((every, width), lambda h, c: (0, h)),
        out_shape=jax.ShapeDtypeStruct((every, heads * width), jnp.bfloat16),
        scratch_shapes=[pltpu.VMEM((every, width), jnp.float32)],
        compiler_params=pltpu.CompilerParams(vmem_limit_bytes=50 * 2**20),
    )(counts, all_queries, all_grads, all_grads, ranks, rank_cols, cluster_keys, values)
    returned = lax.all_to_all(
        partial.reshape(groups, token_count, heads * width), "grp", split_axis=0, concat_axis=0, tiled=True
    )
    return jnp.sum(returned.astype(jnp.float32), axis=0).astype(jnp.bfloat16)


def solution(mesh):
    placed = (
        P("grp", "pb"),
        P("grp", "pb"),
        P("grp", "pb"),
        P("pb", None),
        P("grp", "pb"),
        P("pb", "grp", None),
        P("pb", None),
        P("pb", "grp"),
        P("pb", "grp", None, None),
        P("pb", "grp", None, None),
    )
    return jax.shard_map(shards, mesh=mesh, in_specs=placed, out_specs=P("grp", "pb"), check_vma=False)
```

```python
import functools

import jax
import jax.numpy as jnp
from jax import lax
from jax.experimental import pallas as pl
from jax.experimental.pallas import tpu as pltpu
from jax.sharding import PartitionSpec as P

LANES = 128
AUX = 8
PAIR = 2
CHUNKS = 4
MESH = pl.DeviceIdType.MESH


def three_parts(x):
    high = lax.reduce_precision(x, 8, 7)
    rest = x - high
    middle = lax.reduce_precision(rest, 8, 7)
    return jnp.stack([high, middle, rest - middle], axis=-1)


def probe_ranks(probes, owner_slots, local_clusters, token_count, groups):
    me = lax.axis_index("grp")
    clusters = owner_slots.shape[1]
    cluster_ids = jnp.arange(clusters, dtype=jnp.int32)
    slots = me * local_clusters + jnp.arange(local_clusters, dtype=jnp.int32)
    named = jnp.sum(
        jnp.where(owner_slots[:, None, :] == slots[None, :, None], cluster_ids, 0), axis=2, dtype=jnp.int32
    )
    marked = jnp.any(probes[:, None, :, :] == named[:, :, None, None], axis=3)
    marked = marked.reshape(probes.shape[0], local_clusters, groups, token_count)
    earlier = jnp.arange(token_count)[:, None] < jnp.arange(token_count)[None, :]
    before = lax.dot_general(
        marked.astype(jnp.bfloat16),
        earlier.astype(jnp.bfloat16),
        (((3,), (0,)), ((), ())),
        preferred_element_type=jnp.float32,
    )
    return jnp.where(marked, before.astype(jnp.int32), -1)


def readout_kernel(
    groups, heads, width, r, w, outputs, base, full, rbuf, wbuf, rsend, rrecv, zsend, zrecv, local_sem, wsem
):
    p, z = lax.axis_index("pb"), lax.axis_index("grp")
    token_count, depth = r.shape
    blocks = rbuf.shape[0]
    chunk = token_count // CHUNKS
    half = chunk // 2

    def flip(bit, q):
        return q + bit - 2 * bit * lax.rem(lax.div(q, bit), 2)

    core, across, along = flip(1, p), flip(2, p), flip(4, p)
    corner = flip(4, across)
    has_left, has_right = z > 0, z < groups - 1
    neighbours = jnp.where(has_left, 1, 0) + jnp.where(has_right, 1, 0)

    barrier = pltpu.get_barrier_semaphore()
    for other in (core, across, along):
        pl.semaphore_signal(barrier, inc=1, device_id={"pb": other}, device_id_type=MESH)

    @pl.when(has_left)
    def _():
        pl.semaphore_signal(barrier, inc=1, device_id={"grp": z - 1}, device_id_type=MESH)

    @pl.when(has_right)
    def _():
        pl.semaphore_signal(barrier, inc=1, device_id={"grp": z + 1}, device_id_type=MESH)

    own_block = pltpu.make_async_copy(r, rbuf.at[p], local_sem)
    own_block.start()
    weights = [
        pltpu.make_async_copy(w.at[:, pl.ds(b * depth, depth)], wbuf.at[b], wsem.at[b]) for b in range(blocks)
    ]
    for copy in weights:
        copy.start()
    pl.semaphore_wait(barrier, 3 + neighbours)

    def hop(kind, t, block, target, own=False):
        first = t * chunk + (half if kind in (6, 8) else 0)
        where = pl.ds(first, half if kind in (5, 6, 7, 8) else chunk)
        return pltpu.make_async_remote_copy(
            src_ref=r.at[where] if own else rbuf.at[block, where],
            dst_ref=rbuf.at[block, where],
            send_sem=rsend.at[t, kind],
            recv_sem=rrecv.at[t, kind],
            device_id={"pb": target},
            device_id_type=MESH,
        )

    started = []

    def start(*what, **kw):
        copy = hop(*what, **kw)
        copy.start()
        started.append(copy)

    def send_own(t):
        start(1, t, p, across, own=True)
        start(2, t, p, along, own=True)
        start(0, t, p, core, own=True)

    def zhop(t, source, way):
        where = full.at[source, pl.ds(t * chunk, chunk)]
        return pltpu.make_async_remote_copy(
            src_ref=where,
            dst_ref=where,
            send_sem=zsend.at[t, source, (way + 1) // 2],
            recv_sem=zrecv.at[t, source],
            device_id={"grp": z + way},
            device_id_type=MESH,
        )

    def pass_on(t, distance):
        for way in (1, -1):
            source = z - way * distance
            here = (source >= 0) & (source < groups)
            onward = (z + way >= 0) & (z + way < groups)

            @pl.when(here)
            def _():
                zhop(t, source, way).wait_recv()

            @pl.when(here & onward)
            def _():
                zhop(t, source, way).start()

    def finish(t, distance):
        for way in (1, -1):
            source = z - way * distance

            @pl.when((source >= 0) & (source < groups) & (z + way >= 0) & (z + way < groups))
            def _():
                zhop(t, source, way).wait_send()

    def multiply(t):
        rows = pl.ds(t * chunk, chunk)
        total = jnp.zeros((chunk, wbuf.shape[1]), jnp.float32)
        for b in range(blocks):
            total += lax.dot_general(
                rbuf[b, rows, :], wbuf[b], (((1,), (1,)), ((), ())), preferred_element_type=jnp.float32
            )
        grad = total.astype(jnp.bfloat16)
        product = grad.astype(jnp.float32) * outputs[rows, :].astype(jnp.float32)
        lane = lax.broadcasted_iota(jnp.int32, (chunk, LANES), 1)
        aux = base[rows, :]
        for h in range(heads):
            delta = -jnp.sum(product[:, h * width : (h + 1) * width], axis=1, keepdims=True)
            high = delta.astype(jnp.bfloat16).astype(jnp.float32)
            rest = delta - high
            middle = rest.astype(jnp.bfloat16).astype(jnp.float32)
            for i, part in enumerate((high, middle, rest - middle)):
                aux = jnp.where(lane == h * AUX + 3 + i, part, aux)
        full[z, rows, : heads * width] = grad
        full[z, rows, heads * width :] = aux.astype(jnp.bfloat16)

    send_own(0)
    send_own(1)
    own_block.wait()
    for t in range(CHUNKS + groups - 1):
        if t < CHUNKS:
            hop(1, t, across, across).wait_recv()
            start(5, t, across, along)
            start(3, t, across, core)
            hop(2, t, along, along).wait_recv()
            start(6, t, along, across)
            start(4, t, along, core)
            if t + 2 < CHUNKS:
                send_own(t + 2)
        if 1 <= t <= CHUNKS:
            last = t - 1
            hop(5, last, corner, along).wait_recv()
            start(7, last, corner, core)
            hop(6, last, corner, across).wait_recv()
            start(8, last, corner, core)
        for distance in range(1, groups - 1):
            if 0 <= t - 1 - distance < CHUNKS:
                pass_on(t - 1 - distance, distance)
        if 1 <= t <= CHUNKS:
            if t == 1:
                for copy in weights:
                    copy.wait()
            hop(0, last, core, core).wait_recv()
            hop(3, last, flip(2, core), core).wait_recv()
            hop(4, last, flip(4, core), core).wait_recv()
            hop(7, last, flip(1, corner), core).wait_recv()
            hop(8, last, flip(1, corner), core).wait_recv()
            multiply(last)

            @pl.when(has_right)
            def _():
                zhop(last, z, 1).start()

            @pl.when(has_left)
            def _():
                zhop(last, z, -1).start()

    for t in range(CHUNKS):
        for way in (1, -1):
            source = z - way * (groups - 1)

            @pl.when((source >= 0) & (source < groups))
            def _():
                zhop(t, source, way).wait_recv()

    for copy in started:
        copy.wait_send()
    for t in range(CHUNKS):
        for distance in range(groups - 1):
            finish(t, distance)


def readout(readout_grad, readout_weight, outputs, base, groups, heads, width):
    token_count, depth = readout_grad.shape
    features = readout_weight.shape[0]
    blocks = lax.axis_size("pb")
    columns = features + LANES
    vmem = pl.BlockSpec(memory_space=pltpu.VMEM)
    return pl.pallas_call(
        functools.partial(readout_kernel, groups, heads, width),
        in_specs=[vmem, pl.BlockSpec(memory_space=pl.ANY), vmem, vmem],
        out_specs=vmem,
        out_shape=jax.ShapeDtypeStruct((groups, token_count, columns), jnp.bfloat16),
        scratch_shapes=[
            pltpu.VMEM((blocks, token_count, depth), jnp.bfloat16),
            pltpu.VMEM((blocks, features, depth), jnp.bfloat16),
            pltpu.SemaphoreType.DMA((CHUNKS, 9)),
            pltpu.SemaphoreType.DMA((CHUNKS, 9)),
            pltpu.SemaphoreType.DMA((CHUNKS, groups, 2)),
            pltpu.SemaphoreType.DMA((CHUNKS, groups)),
            pltpu.SemaphoreType.DMA,
            pltpu.SemaphoreType.DMA((blocks,)),
        ],
        compiler_params=pltpu.CompilerParams(
            collective_id=0, has_side_effects=True, vmem_limit_bytes=50 * 2**20
        ),
        cost_estimate=pl.CostEstimate(
            flops=2 * token_count * features * depth * blocks, bytes_accessed=32 * 2**20, transcendentals=0
        ),
    )(readout_grad, readout_weight, outputs, base)


def grad_kernel(groups, capacity, scale, counts, q, g, aux, rows, cols, keys, values, out, total):
    head, step = pl.program_id(0), pl.program_id(1)
    token_count = q.shape[0] // groups
    span = keys.shape[2]
    lane = lax.broadcasted_iota(jnp.int32, (span, LANES), 1)
    key_id = lax.broadcasted_iota(jnp.int32, (span, LANES), 0)
    own = lane - head * AUX
    ones = jnp.where((own >= 0) & (own < 3), 1.0, 0.0)
    value_side = jnp.where((own >= 3) & (own < 6), 1.0, 0.0).astype(jnp.bfloat16)
    place = lax.broadcasted_iota(jnp.int32, (capacity, token_count), 0)
    contract_last = (((1,), (1,)), ((), ()))
    partials = []
    for i in range(PAIR):
        valid = counts[head, step * PAIR + i]
        key_side = jnp.where((lane == LANES - 1) & (key_id >= valid), -1e30, ones).astype(jnp.bfloat16)
        key_block, value_block = keys[0, i], values[0, i]
        picked = []
        for group in range(groups):
            span_of = pl.ds(group * token_count, token_count)
            chosen = (rows[0, i, :, span_of] == place).astype(jnp.bfloat16)
            rhs = jnp.concatenate([q[span_of, :], aux[span_of, :], g[span_of, :]], axis=1)
            picked.append(jnp.dot(chosen, rhs, preferred_element_type=jnp.float32).astype(jnp.bfloat16))
        picked = jnp.concatenate(picked, axis=0)
        scores = lax.dot_general(
            picked[:, : 2 * LANES],
            jnp.concatenate([key_block, key_side], axis=1),
            contract_last,
            preferred_element_type=jnp.float32,
        )
        grad_prob = lax.dot_general(
            picked[:, LANES:],
            jnp.concatenate([value_side, value_block], axis=1),
            contract_last,
            preferred_element_type=jnp.float32,
        )
        grad_score = (jnp.exp(scores * scale) * grad_prob).astype(jnp.bfloat16)
        partials.append(jnp.dot(grad_score, key_block, preferred_element_type=jnp.float32).astype(jnp.bfloat16))
    spot = lax.broadcasted_iota(jnp.int32, (token_count, capacity), 1)
    for group in range(groups):
        span_of = pl.ds(group * token_count, token_count)
        chosen = jnp.concatenate(
            [(cols[0, 0, span_of, i : i + 1] == spot).astype(jnp.bfloat16) for i in range(PAIR)], axis=1
        )
        part = jnp.concatenate([p[group * capacity : (group + 1) * capacity] for p in partials], axis=0)
        add = jnp.dot(chosen, part, preferred_element_type=jnp.float32)

        @pl.when(step == 0)
        def _():
            total[span_of, :] = add

        @pl.when(step > 0)
        def _():
            total[span_of, :] += add

    @pl.when(step == pl.num_programs(1) - 1)
    def _():
        out[...] = (total[...] * scale).astype(out.dtype)


def shards(
    queries, outputs, readout_grad, readout_weight, log_norm, probes, owner_slots, counts, cluster_keys, values
):
    token_count = queries.shape[0]
    heads, local_clusters, span, width = cluster_keys.shape
    clusters = owner_slots.shape[1]
    groups = lax.axis_size("grp")
    capacity = 2 * token_count * probes.shape[2] // clusters
    scale = width ** (-0.5)
    every = groups * token_count

    steps = local_clusters // PAIR
    probe_lanes = probes.transpose(1, 0, 2).reshape(token_count, heads * probes.shape[2])
    probe_lanes = jnp.pad(probe_lanes, ((0, 0), (0, LANES - probe_lanes.shape[1]))).astype(jnp.bfloat16)
    all_queries = lax.all_gather(jnp.concatenate([queries, probe_lanes], axis=1), "grp", axis=0, tiled=True)
    base = jnp.concatenate(
        [three_parts(log_norm * (-1.0 / scale)), jnp.zeros((token_count, heads, AUX - 3))], axis=2
    ).reshape(token_count, heads * AUX)
    base = jnp.concatenate(
        [base, jnp.zeros((token_count, LANES - 1 - heads * AUX)), jnp.ones((token_count, 1))], axis=1
    )

    if groups == 4 and lax.axis_size("pb") == 8:
        all_grads = readout(readout_grad, readout_weight, outputs, base, groups, heads, width)
        all_grads = all_grads.reshape(every, heads * width + LANES)
    else:
        grad_out = lax.dot_general(
            lax.all_gather(readout_grad, "pb", axis=1, tiled=True),
            readout_weight,
            (((1,), (1,)), ((), ())),
            preferred_element_type=jnp.float32,
        ).astype(jnp.bfloat16)
        row_delta = jnp.sum(
            (grad_out.astype(jnp.float32) * outputs.astype(jnp.float32)).reshape(token_count, heads, width), axis=2
        )
        deltas = jnp.pad(three_parts(-row_delta), ((0, 0), (0, 0), (3, AUX - 6))).reshape(token_count, heads * AUX)
        aux = base + jnp.pad(deltas, ((0, 0), (0, LANES - heads * AUX)))
        all_grads = lax.all_gather(
            jnp.concatenate([grad_out, aux.astype(jnp.bfloat16)], axis=1), "grp", axis=0, tiled=True
        )

    all_probes = all_queries[:, heads * width : heads * width + heads * probes.shape[2]].astype(jnp.int32)
    all_probes = all_probes.reshape(every, heads, probes.shape[2]).transpose(1, 0, 2)
    ranks = probe_ranks(all_probes, owner_slots, local_clusters, token_count, groups)
    ranks = ranks.reshape(heads, local_clusters, 1, every)
    rank_cols = ranks.reshape(heads, steps, PAIR, every).transpose(0, 1, 3, 2)

    partial = pl.pallas_call(
        functools.partial(grad_kernel, groups, capacity, scale),
        grid=(heads, steps),
        in_specs=[
            pl.BlockSpec(memory_space=pltpu.SMEM),
            pl.BlockSpec((every, width), lambda h, c: (0, h)),
            pl.BlockSpec((every, width), lambda h, c: (0, h)),
            pl.BlockSpec((every, LANES), lambda h, c: (0, heads)),
            pl.BlockSpec((1, PAIR, 1, every), lambda h, c: (h, c, 0, 0)),
            pl.BlockSpec((1, 1, every, PAIR), lambda h, c: (h, c, 0, 0)),
            pl.BlockSpec((1, PAIR, span, width), lambda h, c: (h, c, 0, 0)),
            pl.BlockSpec((1, PAIR, span, width), lambda h, c: (h, c, 0, 0)),
        ],
        out_specs=pl.BlockSpec((every, width), lambda h, c: (0, h)),
        out_shape=jax.ShapeDtypeStruct((every, heads * width), jnp.bfloat16),
        scratch_shapes=[pltpu.VMEM((every, width), jnp.float32)],
        compiler_params=pltpu.CompilerParams(vmem_limit_bytes=50 * 2**20),
    )(counts, all_queries, all_grads, all_grads, ranks, rank_cols, cluster_keys, values)
    returned = lax.all_to_all(
        partial.reshape(groups, token_count, heads * width), "grp", split_axis=0, concat_axis=0, tiled=True
    )
    return jnp.sum(returned.astype(jnp.float32), axis=0).astype(jnp.bfloat16)


def solution(mesh):
    placed = (
        P("grp", "pb"),
        P("grp", "pb"),
        P("grp", "pb"),
        P("pb", None),
        P("grp", "pb"),
        P("pb", "grp", None),
        P("pb", None),
        P("pb", "grp"),
        P("pb", "grp", None, None),
        P("pb", "grp", None, None),
    )
    return jax.shard_map(shards, mesh=mesh, in_specs=placed, out_specs=P("grp", "pb"), check_vma=False)
```

```python
import functools

import jax
import jax.numpy as jnp
from jax import lax
from jax.experimental import pallas as pl
from jax.experimental.pallas import tpu as pltpu
from jax.sharding import PartitionSpec as P

LANES = 128
AUX = 8
PAIR = 2
CHUNKS = 4
MESH = pl.DeviceIdType.MESH


def three_parts(x):
    high = lax.reduce_precision(x, 8, 7)
    rest = x - high
    middle = lax.reduce_precision(rest, 8, 7)
    return jnp.stack([high, middle, rest - middle], axis=-1)


def named_clusters(owner_slots, local_clusters):
    cluster_ids = jnp.arange(owner_slots.shape[1], dtype=jnp.int32)
    slots = lax.axis_index("grp") * local_clusters + jnp.arange(local_clusters, dtype=jnp.int32)
    return jnp.sum(jnp.where(owner_slots[:, None, :] == slots[None, :, None], cluster_ids, 0), axis=2, dtype=jnp.int32)


def probe_ranks(probes, named, token_count, groups):
    local_clusters = named.shape[1]
    marked = jnp.any(probes[:, None, :, :] == named[:, :, None, None], axis=3)
    marked = marked.reshape(probes.shape[0], local_clusters, groups, token_count)
    earlier = jnp.arange(token_count)[:, None] < jnp.arange(token_count)[None, :]
    before = lax.dot_general(
        marked.astype(jnp.bfloat16),
        earlier.astype(jnp.bfloat16),
        (((3,), (0,)), ((), ())),
        preferred_element_type=jnp.float32,
    )
    return jnp.where(marked, before.astype(jnp.int32), -1)


def readout_kernel(
    groups, heads, width, r, w, outputs, base, q, probes, named, full, qall, rows_out, cols_out, rbuf, wbuf, pbuf,
    rsend, rrecv, zsend, zrecv, local_sem, wsem
):
    p, z = lax.axis_index("pb"), lax.axis_index("grp")
    token_count, depth = r.shape
    blocks = rbuf.shape[0]
    chunk = token_count // CHUNKS
    half = chunk // 2

    def flip(bit, q):
        return q + bit - 2 * bit * lax.rem(lax.div(q, bit), 2)

    core, across, along = flip(1, p), flip(2, p), flip(4, p)
    corner = flip(4, across)
    has_left, has_right = z > 0, z < groups - 1
    neighbours = jnp.where(has_left, 1, 0) + jnp.where(has_right, 1, 0)

    barrier = pltpu.get_barrier_semaphore()
    for other in (core, across, along):
        pl.semaphore_signal(barrier, inc=1, device_id={"pb": other}, device_id_type=MESH)

    @pl.when(has_left)
    def _():
        pl.semaphore_signal(barrier, inc=1, device_id={"grp": z - 1}, device_id_type=MESH)

    @pl.when(has_right)
    def _():
        pl.semaphore_signal(barrier, inc=1, device_id={"grp": z + 1}, device_id_type=MESH)

    own_block = pltpu.make_async_copy(r, rbuf.at[p], local_sem)
    own_block.start()
    weights = [
        pltpu.make_async_copy(w.at[:, pl.ds(b * depth, depth)], wbuf.at[b], wsem.at[b]) for b in range(blocks)
    ]
    for copy in weights:
        copy.start()
    pl.semaphore_wait(barrier, 3 + neighbours)

    def hop(kind, t, block, target, own=False):
        first = t * chunk + (half if kind in (6, 8) else 0)
        where = pl.ds(first, half if kind in (5, 6, 7, 8) else chunk)
        return pltpu.make_async_remote_copy(
            src_ref=r.at[where] if own else rbuf.at[block, where],
            dst_ref=rbuf.at[block, where],
            send_sem=rsend.at[t, kind],
            recv_sem=rrecv.at[t, kind],
            device_id={"pb": target},
            device_id_type=MESH,
        )

    started = []

    def start(*what, **kw):
        copy = hop(*what, **kw)
        copy.start()
        started.append(copy)

    def send_own(t):
        start(1, t, p, across, own=True)
        start(2, t, p, along, own=True)
        start(0, t, p, core, own=True)

    def zhop(t, source, way):
        if t < CHUNKS:
            where = full.at[source, pl.ds(t * chunk, chunk)]
        elif t < 2 * CHUNKS:
            where = qall.at[source, pl.ds((t - CHUNKS) * chunk, chunk)]
        else:
            where = pbuf.at[source]
        return pltpu.make_async_remote_copy(
            src_ref=where,
            dst_ref=where,
            send_sem=zsend.at[t, source, (way + 1) // 2],
            recv_sem=zrecv.at[t, source],
            device_id={"grp": z + way},
            device_id_type=MESH,
        )

    def pass_on(t, distance):
        for way in (1, -1):
            source = z - way * distance
            here = (source >= 0) & (source < groups)
            onward = (z + way >= 0) & (z + way < groups)

            @pl.when(here)
            def _():
                zhop(t, source, way).wait_recv()

            @pl.when(here & onward)
            def _():
                zhop(t, source, way).start()

    def finish(t, distance):
        for way in (1, -1):
            source = z - way * distance

            @pl.when((source >= 0) & (source < groups) & (z + way >= 0) & (z + way < groups))
            def _():
                zhop(t, source, way).wait_send()

    def multiply(t):
        rows = pl.ds(t * chunk, chunk)
        total = jnp.zeros((chunk, wbuf.shape[1]), jnp.float32)
        for b in range(blocks):
            total += lax.dot_general(
                rbuf[b, rows, :], wbuf[b], (((1,), (1,)), ((), ())), preferred_element_type=jnp.float32
            )
        grad = total.astype(jnp.bfloat16)
        product = grad.astype(jnp.float32) * outputs[rows, :].astype(jnp.float32)
        lane = lax.broadcasted_iota(jnp.int32, (chunk, LANES), 1)
        aux = base[rows, :]
        for h in range(heads):
            delta = -jnp.sum(product[:, h * width : (h + 1) * width], axis=1, keepdims=True)
            high = delta.astype(jnp.bfloat16).astype(jnp.float32)
            rest = delta - high
            middle = rest.astype(jnp.bfloat16).astype(jnp.float32)
            for i, part in enumerate((high, middle, rest - middle)):
                aux = jnp.where(lane == h * AUX + 3 + i, part, aux)
        full[z, rows, : heads * width] = grad
        full[z, rows, heads * width :] = aux.astype(jnp.bfloat16)

    def zsend_own(t):
        @pl.when(has_right)
        def _():
            zhop(t, z, 1).start()

        @pl.when(has_left)
        def _():
            zhop(t, z, -1).start()

    def zlast(t):
        for way in (1, -1):
            source = z - way * (groups - 1)

            @pl.when((source >= 0) & (source < groups))
            def _():
                zhop(t, source, way).wait_recv()

    def rank():
        earlier = lax.broadcasted_iota(jnp.int32, (token_count, token_count), 0) < lax.broadcasted_iota(
            jnp.int32, (token_count, token_count), 1
        )
        earlier = earlier.astype(jnp.bfloat16)
        local = named.shape[0] // heads
        count = pbuf.shape[1] // heads
        for group in range(groups):
            marked = []
            for h in range(heads):
                ids = named[h * local : (h + 1) * local, :]
                hit = jnp.zeros((local, token_count), jnp.float32)
                for j in range(count):
                    at = h * count + j
                    hit += jnp.where(pbuf[group, at : at + 1, :] == ids, 1.0, 0.0)
                marked.append(hit)
            marked = jnp.concatenate(marked, axis=0)
            before = jnp.dot(marked.astype(jnp.bfloat16), earlier, preferred_element_type=jnp.float32)
            ranks = jnp.where(marked > 0.5, before, -1.0)
            rows_out[group] = ranks.astype(jnp.int32)
            padded = jnp.concatenate([ranks, jnp.zeros((LANES - ranks.shape[0], token_count), jnp.float32)], axis=0)
            cols_out[group] = padded.T.astype(jnp.int32)

    qall[z] = q[...]
    pbuf[z] = probes[...]
    send_own(0)
    for t in (2 * CHUNKS, *range(CHUNKS, 2 * CHUNKS)):
        zsend_own(t)
    send_own(1)
    own_block.wait()
    for t in range(CHUNKS + groups - 1):
        if t < CHUNKS:
            hop(1, t, across, across).wait_recv()
            start(5, t, across, along)
            start(3, t, across, core)
            hop(2, t, along, along).wait_recv()
            start(6, t, along, across)
            start(4, t, along, core)
            if t + 2 < CHUNKS:
                send_own(t + 2)
        if 1 <= t <= CHUNKS:
            last = t - 1
            hop(5, last, corner, along).wait_recv()
            start(7, last, corner, core)
            hop(6, last, corner, across).wait_recv()
            start(8, last, corner, core)
        early = {0: [8, 4, 5, 6], 1: [7, 8, 4, 5, 6], 2: [7]}.get(t, [])
        for k, piece in enumerate(early):
            pass_on(piece, 1 if t == 0 or (t == 1 and k == 0) else 2)
        for distance in range(1, groups - 1):
            if 0 <= t - 1 - distance < CHUNKS:
                pass_on(t - 1 - distance, distance)
        if 1 <= t <= CHUNKS:
            if t == 1:
                for copy in weights:
                    copy.wait()
            hop(0, last, core, core).wait_recv()
            hop(3, last, flip(2, core), core).wait_recv()
            hop(4, last, flip(4, core), core).wait_recv()
            hop(7, last, flip(1, corner), core).wait_recv()
            hop(8, last, flip(1, corner), core).wait_recv()
            multiply(last)
            zsend_own(last)
        if t == 2:
            zlast(2 * CHUNKS)
            rank()

    for t in range(2 * CHUNKS):
        zlast(t)

    for copy in started:
        copy.wait_send()
    for t in range(2 * CHUNKS + 1):
        for distance in range(groups - 1):
            finish(t, distance)


def readout(readout_grad, readout_weight, outputs, base, queries, probes, named, groups, heads, width):
    token_count, depth = readout_grad.shape
    features = readout_weight.shape[0]
    blocks = lax.axis_size("pb")
    vmem = pl.BlockSpec(memory_space=pltpu.VMEM)
    pieces = 2 * CHUNKS + 1
    return pl.pallas_call(
        functools.partial(readout_kernel, groups, heads, width),
        in_specs=[vmem, pl.BlockSpec(memory_space=pl.ANY), vmem, vmem, vmem, vmem, vmem],
        out_specs=[vmem] * 4,
        out_shape=[
            jax.ShapeDtypeStruct((groups, token_count, features + LANES), jnp.bfloat16),
            jax.ShapeDtypeStruct((groups, token_count, features), jnp.bfloat16),
            jax.ShapeDtypeStruct((groups, named.shape[0], token_count), jnp.int32),
            jax.ShapeDtypeStruct((groups, token_count, LANES), jnp.int32),
        ],
        scratch_shapes=[
            pltpu.VMEM((blocks, token_count, depth), jnp.bfloat16),
            pltpu.VMEM((blocks, features, depth), jnp.bfloat16),
            pltpu.VMEM((groups,) + probes.shape, jnp.int32),
            pltpu.SemaphoreType.DMA((CHUNKS, 9)),
            pltpu.SemaphoreType.DMA((CHUNKS, 9)),
            pltpu.SemaphoreType.DMA((pieces, groups, 2)),
            pltpu.SemaphoreType.DMA((pieces, groups)),
            pltpu.SemaphoreType.DMA,
            pltpu.SemaphoreType.DMA((blocks,)),
        ],
        compiler_params=pltpu.CompilerParams(
            collective_id=0, has_side_effects=True, vmem_limit_bytes=50 * 2**20
        ),
        cost_estimate=pl.CostEstimate(
            flops=2 * token_count * features * depth * blocks, bytes_accessed=32 * 2**20, transcendentals=0
        ),
    )(readout_grad, readout_weight, outputs, base, queries, probes, named)


def attend_kernel(
    groups, capacity, scale, counts, q, g, rows, cols, keys, values, out,
    kbuf, vbuf, turned, partials, outgoing, arrived, ksem, vsem, ssem, rsem
):
    me = lax.axis_index("grp")
    heads, local, span, width = kbuf.shape
    token_count = q.shape[1]
    contract_last = (((1,), (1,)), ((), ()))

    barrier = pltpu.get_barrier_semaphore()
    for d in range(1, groups):
        pl.semaphore_signal(
            barrier, inc=1, device_id={"grp": lax.rem(me + d, groups)}, device_id_type=MESH
        )

    def loads(h):
        return (
            pltpu.make_async_copy(keys.at[h], kbuf.at[h], ksem.at[h]),
            pltpu.make_async_copy(values.at[h], vbuf.at[h], vsem.at[h]),
        )

    def home(h, d):
        there = lax.rem(me + d, groups)
        return pltpu.make_async_remote_copy(
            src_ref=outgoing.at[h, there],
            dst_ref=arrived.at[h, d - 1],
            send_sem=ssem.at[h, d - 1],
            recv_sem=rsem.at[h, d - 1],
            device_id={"grp": there},
            device_id_type=MESH,
        )

    for h in range(heads):
        for copy in loads(h):
            copy.start()
    pl.semaphore_wait(barrier, groups - 1)

    lane = lax.broadcasted_iota(jnp.int32, (span, LANES), 1)
    key_id = lax.broadcasted_iota(jnp.int32, (span, LANES), 0)
    place = lax.broadcasted_iota(jnp.int32, (capacity, token_count), 0)
    spot = lax.broadcasted_iota(jnp.int32, (token_count, capacity), 1)

    def one_head(h, carry):
        for copy in loads(h):
            copy.wait()
        own = lane - h * AUX
        ones = jnp.where((own >= 0) & (own < 3), 1.0, 0.0)
        value_side = jnp.where((own >= 3) & (own < 6), 1.0, 0.0).astype(jnp.bfloat16)
        columns = pl.ds(pl.multiple_of(h * width, width), width)
        aux_at = heads * width
        for c in range(local):
            valid = counts[h, c]
            key_side = jnp.where((lane == LANES - 1) & (key_id >= valid), -1e30, ones).astype(jnp.bfloat16)
            picked = []
            for group in range(groups):
                chosen = (rows[group, pl.ds(h * local + c, 1), :] == place).astype(jnp.bfloat16)
                rhs = jnp.concatenate(
                    [q[group, :, columns], g[group, :, aux_at : aux_at + LANES], g[group, :, columns]], axis=1
                )
                picked.append(jnp.dot(chosen, rhs, preferred_element_type=jnp.float32).astype(jnp.bfloat16))
            picked = jnp.concatenate(picked, axis=0)
            key_block, value_block = kbuf[h, c], vbuf[h, c]
            scores = lax.dot_general(
                picked[:, : 2 * LANES],
                jnp.concatenate([key_block, key_side], axis=1),
                contract_last,
                preferred_element_type=jnp.float32,
            )
            grad_prob = lax.dot_general(
                picked[:, LANES:],
                jnp.concatenate([value_side, value_block], axis=1),
                contract_last,
                preferred_element_type=jnp.float32,
            )
            grad_score = (jnp.exp(scores * scale) * grad_prob).astype(jnp.bfloat16)
            part = jnp.dot(grad_score, key_block, preferred_element_type=jnp.float32).astype(jnp.bfloat16)
            for group in range(groups):
                partials[group, c * capacity : (c + 1) * capacity, :] = part[
                    group * capacity : (group + 1) * capacity
                ]
        for group in range(groups):
            turned[...] = pltpu.roll(cols[group], lax.rem(LANES - h * local, LANES), 1)
            chosen = jnp.concatenate(
                [(turned[:, c : c + 1] == spot).astype(jnp.bfloat16) for c in range(local)], axis=1
            )
            total = jnp.dot(chosen, partials[group], preferred_element_type=jnp.float32)
            outgoing[h, group] = (total * scale).astype(jnp.bfloat16)
        for d in range(1, groups):
            home(h, d).start()
        return carry

    lax.fori_loop(0, heads, one_head, 0)
    for h in range(heads):
        total = outgoing[h, me].astype(jnp.float32)
        for d in range(1, groups):
            home(h, d).wait_recv()
            total += arrived[h, d - 1].astype(jnp.float32)
        out[:, h * width : (h + 1) * width] = total.astype(out.dtype)
    for h in range(heads):
        for d in range(1, groups):
            home(h, d).wait_send()


def attend(counts, q, g, rows, cols, keys, values, capacity, scale):
    groups, token_count, features = q.shape
    heads, local, span, width = keys.shape
    vmem = pl.BlockSpec(memory_space=pltpu.VMEM)
    hbm = pl.BlockSpec(memory_space=pl.ANY)
    return pl.pallas_call(
        functools.partial(attend_kernel, groups, capacity, scale),
        in_specs=[pl.BlockSpec(memory_space=pltpu.SMEM), vmem, vmem, vmem, vmem, hbm, hbm],
        out_specs=vmem,
        out_shape=jax.ShapeDtypeStruct((token_count, features), jnp.bfloat16),
        scratch_shapes=[
            pltpu.VMEM(keys.shape, jnp.bfloat16),
            pltpu.VMEM(values.shape, jnp.bfloat16),
            pltpu.VMEM((token_count, LANES), jnp.int32),
            pltpu.VMEM((groups, local * capacity, width), jnp.bfloat16),
            pltpu.VMEM((heads, groups, token_count, width), jnp.bfloat16),
            pltpu.VMEM((heads, groups - 1, token_count, width), jnp.bfloat16),
            pltpu.SemaphoreType.DMA((heads,)),
            pltpu.SemaphoreType.DMA((heads,)),
            pltpu.SemaphoreType.DMA((heads, groups - 1)),
            pltpu.SemaphoreType.DMA((heads, groups - 1)),
        ],
        compiler_params=pltpu.CompilerParams(
            collective_id=1, has_side_effects=True, vmem_limit_bytes=50 * 2**20
        ),
    )(counts, q, g, rows, cols, keys, values)


def grad_kernel(groups, capacity, scale, counts, q, g, aux, rows, cols, keys, values, out, total):
    head, step = pl.program_id(0), pl.program_id(1)
    token_count = q.shape[0] // groups
    span = keys.shape[2]
    lane = lax.broadcasted_iota(jnp.int32, (span, LANES), 1)
    key_id = lax.broadcasted_iota(jnp.int32, (span, LANES), 0)
    own = lane - head * AUX
    ones = jnp.where((own >= 0) & (own < 3), 1.0, 0.0)
    value_side = jnp.where((own >= 3) & (own < 6), 1.0, 0.0).astype(jnp.bfloat16)
    place = lax.broadcasted_iota(jnp.int32, (capacity, token_count), 0)
    contract_last = (((1,), (1,)), ((), ()))
    partials = []
    for i in range(PAIR):
        valid = counts[head, step * PAIR + i]
        key_side = jnp.where((lane == LANES - 1) & (key_id >= valid), -1e30, ones).astype(jnp.bfloat16)
        key_block, value_block = keys[0, i], values[0, i]
        picked = []
        for group in range(groups):
            span_of = pl.ds(group * token_count, token_count)
            chosen = (rows[0, i, :, span_of] == place).astype(jnp.bfloat16)
            rhs = jnp.concatenate([q[span_of, :], aux[span_of, :], g[span_of, :]], axis=1)
            picked.append(jnp.dot(chosen, rhs, preferred_element_type=jnp.float32).astype(jnp.bfloat16))
        picked = jnp.concatenate(picked, axis=0)
        scores = lax.dot_general(
            picked[:, : 2 * LANES],
            jnp.concatenate([key_block, key_side], axis=1),
            contract_last,
            preferred_element_type=jnp.float32,
        )
        grad_prob = lax.dot_general(
            picked[:, LANES:],
            jnp.concatenate([value_side, value_block], axis=1),
            contract_last,
            preferred_element_type=jnp.float32,
        )
        grad_score = (jnp.exp(scores * scale) * grad_prob).astype(jnp.bfloat16)
        partials.append(jnp.dot(grad_score, key_block, preferred_element_type=jnp.float32).astype(jnp.bfloat16))
    spot = lax.broadcasted_iota(jnp.int32, (token_count, capacity), 1)
    for group in range(groups):
        span_of = pl.ds(group * token_count, token_count)
        chosen = jnp.concatenate(
            [(cols[0, 0, span_of, i : i + 1] == spot).astype(jnp.bfloat16) for i in range(PAIR)], axis=1
        )
        part = jnp.concatenate([p[group * capacity : (group + 1) * capacity] for p in partials], axis=0)
        add = jnp.dot(chosen, part, preferred_element_type=jnp.float32)

        @pl.when(step == 0)
        def _():
            total[span_of, :] = add

        @pl.when(step > 0)
        def _():
            total[span_of, :] += add

    @pl.when(step == pl.num_programs(1) - 1)
    def _():
        out[...] = (total[...] * scale).astype(out.dtype)


def shards(
    queries, outputs, readout_grad, readout_weight, log_norm, probes, owner_slots, counts, cluster_keys, values
):
    token_count = queries.shape[0]
    heads, local_clusters, span, width = cluster_keys.shape
    clusters = owner_slots.shape[1]
    groups = lax.axis_size("grp")
    capacity = 2 * token_count * probes.shape[2] // clusters
    scale = width ** (-0.5)
    every = groups * token_count

    steps = local_clusters // PAIR
    named = named_clusters(owner_slots, local_clusters)
    base = jnp.concatenate(
        [three_parts(log_norm * (-1.0 / scale)), jnp.zeros((token_count, heads, AUX - 3))], axis=2
    ).reshape(token_count, heads * AUX)
    base = jnp.concatenate(
        [base, jnp.zeros((token_count, LANES - 1 - heads * AUX)), jnp.ones((token_count, 1))], axis=1
    )

    if groups == 4 and lax.axis_size("pb") == 8:
        all_grads, all_queries, rows, cols = readout(
            readout_grad,
            readout_weight,
            outputs,
            base,
            queries,
            probes.transpose(0, 2, 1).reshape(heads * probes.shape[2], token_count),
            named.reshape(heads * local_clusters, 1),
            groups,
            heads,
            width,
        )
        return attend(counts, all_queries, all_grads, rows, cols, cluster_keys, values, capacity, scale)

    probe_lanes = probes.transpose(1, 0, 2).reshape(token_count, heads * probes.shape[2])
    probe_lanes = jnp.pad(probe_lanes, ((0, 0), (0, LANES - probe_lanes.shape[1]))).astype(jnp.bfloat16)
    all_queries = lax.all_gather(jnp.concatenate([queries, probe_lanes], axis=1), "grp", axis=0, tiled=True)
    grad_out = lax.dot_general(
        lax.all_gather(readout_grad, "pb", axis=1, tiled=True),
        readout_weight,
        (((1,), (1,)), ((), ())),
        preferred_element_type=jnp.float32,
    ).astype(jnp.bfloat16)
    row_delta = jnp.sum(
        (grad_out.astype(jnp.float32) * outputs.astype(jnp.float32)).reshape(token_count, heads, width), axis=2
    )
    deltas = jnp.pad(three_parts(-row_delta), ((0, 0), (0, 0), (3, AUX - 6))).reshape(token_count, heads * AUX)
    aux = base + jnp.pad(deltas, ((0, 0), (0, LANES - heads * AUX)))
    all_grads = lax.all_gather(
        jnp.concatenate([grad_out, aux.astype(jnp.bfloat16)], axis=1), "grp", axis=0, tiled=True
    )

    all_probes = all_queries[:, heads * width : heads * width + heads * probes.shape[2]].astype(jnp.int32)
    all_probes = all_probes.reshape(every, heads, probes.shape[2]).transpose(1, 0, 2)
    ranks = probe_ranks(all_probes, named, token_count, groups)
    ranks = ranks.reshape(heads, local_clusters, 1, every)
    rank_cols = ranks.reshape(heads, steps, PAIR, every).transpose(0, 1, 3, 2)

    partial = pl.pallas_call(
        functools.partial(grad_kernel, groups, capacity, scale),
        grid=(heads, steps),
        in_specs=[
            pl.BlockSpec(memory_space=pltpu.SMEM),
            pl.BlockSpec((every, width), lambda h, c: (0, h)),
            pl.BlockSpec((every, width), lambda h, c: (0, h)),
            pl.BlockSpec((every, LANES), lambda h, c: (0, heads)),
            pl.BlockSpec((1, PAIR, 1, every), lambda h, c: (h, c, 0, 0)),
            pl.BlockSpec((1, 1, every, PAIR), lambda h, c: (h, c, 0, 0)),
            pl.BlockSpec((1, PAIR, span, width), lambda h, c: (h, c, 0, 0)),
            pl.BlockSpec((1, PAIR, span, width), lambda h, c: (h, c, 0, 0)),
        ],
        out_specs=pl.BlockSpec((every, width), lambda h, c: (0, h)),
        out_shape=jax.ShapeDtypeStruct((every, heads * width), jnp.bfloat16),
        scratch_shapes=[pltpu.VMEM((every, width), jnp.float32)],
        compiler_params=pltpu.CompilerParams(vmem_limit_bytes=50 * 2**20),
    )(counts, all_queries, all_grads, all_grads, ranks, rank_cols, cluster_keys, values)
    returned = lax.all_to_all(
        partial.reshape(groups, token_count, heads * width), "grp", split_axis=0, concat_axis=0, tiled=True
    )
    return jnp.sum(returned.astype(jnp.float32), axis=0).astype(jnp.bfloat16)


def solution(mesh):
    placed = (
        P("grp", "pb"),
        P("grp", "pb"),
        P("grp", "pb"),
        P("pb", None),
        P("grp", "pb"),
        P("pb", "grp", None),
        P("pb", None),
        P("pb", "grp"),
        P("pb", "grp", None, None),
        P("pb", "grp", None, None),
    )
    return jax.shard_map(shards, mesh=mesh, in_specs=placed, out_specs=P("grp", "pb"), check_vma=False)
```

```python
import functools

import jax
import jax.numpy as jnp
from jax import lax
from jax.experimental import pallas as pl
from jax.experimental.pallas import tpu as pltpu
from jax.sharding import PartitionSpec as P

LANES = 128
AUX = 8
PAIR = 2
CHUNKS = 4
MESH = pl.DeviceIdType.MESH
PASSES = {0: ((4, 1), (0, 1), (1, 1)), 1: ((2, 1), (3, 1), (4, 2), (0, 2)), 2: ((1, 2), (2, 2), (3, 2))}


def three_parts(x):
    high = lax.reduce_precision(x, 8, 7)
    rest = x - high
    middle = lax.reduce_precision(rest, 8, 7)
    return jnp.stack([high, middle, rest - middle], axis=-1)


def named_clusters(owner_slots, local_clusters):
    cluster_ids = jnp.arange(owner_slots.shape[1], dtype=jnp.int32)
    slots = lax.axis_index("grp") * local_clusters + jnp.arange(local_clusters, dtype=jnp.int32)
    return jnp.sum(jnp.where(owner_slots[:, None, :] == slots[None, :, None], cluster_ids, 0), axis=2, dtype=jnp.int32)


def probe_ranks(probes, named, token_count, groups):
    local_clusters = named.shape[1]
    marked = jnp.any(probes[:, None, :, :] == named[:, :, None, None], axis=3)
    marked = marked.reshape(probes.shape[0], local_clusters, groups, token_count)
    earlier = jnp.arange(token_count)[:, None] < jnp.arange(token_count)[None, :]
    before = lax.dot_general(
        marked.astype(jnp.bfloat16),
        earlier.astype(jnp.bfloat16),
        (((3,), (0,)), ((), ())),
        preferred_element_type=jnp.float32,
    )
    return jnp.where(marked, before.astype(jnp.int32), -1)


def line(groups, z, place, zsend, zrecv):
    def hop(piece, source, way):
        where = place(piece, source)
        return pltpu.make_async_remote_copy(
            src_ref=where,
            dst_ref=where,
            send_sem=zsend.at[piece, source, (way + 1) // 2],
            recv_sem=zrecv.at[piece, source],
            device_id={"grp": z + way},
            device_id_type=MESH,
        )

    def inside(q):
        return (q >= 0) & (q < groups)

    def send_own(piece):
        for way in (1, -1):

            @pl.when(inside(z + way))
            def _():
                hop(piece, z, way).start()

    def pass_on(piece, distance):
        for way in (1, -1):
            source = z - way * distance

            @pl.when(inside(source))
            def _():
                hop(piece, source, way).wait_recv()

            @pl.when(inside(source) & inside(z + way))
            def _():
                hop(piece, source, way).start()

    def finish(piece):
        for distance in range(groups - 1):
            for way in (1, -1):
                source = z - way * distance

                @pl.when(inside(source) & inside(z + way))
                def _():
                    hop(piece, source, way).wait_send()

    return send_own, pass_on, finish


def readout_kernel(
    groups, heads, width, r, w, outputs, base, q, probes, named, grads, aux_rows, qall, rows_out, cols_out, rbuf, wbuf, pbuf,
    rsend, rrecv, zsend, zrecv, local_sem, wsem
):
    p, z = lax.axis_index("pb"), lax.axis_index("grp")
    token_count, depth = r.shape
    blocks = rbuf.shape[0]
    chunk = token_count // CHUNKS
    half = chunk // 2

    def flip(bit, q):
        return q + bit - 2 * bit * lax.rem(lax.div(q, bit), 2)

    core, across, along = flip(1, p), flip(2, p), flip(4, p)
    corner = flip(4, across)
    has_left, has_right = z > 0, z < groups - 1
    neighbours = jnp.where(has_left, 1, 0) + jnp.where(has_right, 1, 0)

    barrier = pltpu.get_barrier_semaphore()
    for other in (core, across, along):
        pl.semaphore_signal(barrier, inc=1, device_id={"pb": other}, device_id_type=MESH)

    @pl.when(has_left)
    def _():
        pl.semaphore_signal(barrier, inc=1, device_id={"grp": z - 1}, device_id_type=MESH)

    @pl.when(has_right)
    def _():
        pl.semaphore_signal(barrier, inc=1, device_id={"grp": z + 1}, device_id_type=MESH)

    own_block = pltpu.make_async_copy(r, rbuf.at[p], local_sem)
    own_block.start()
    weights = [
        pltpu.make_async_copy(w.at[:, pl.ds(b * depth, depth)], wbuf.at[b], wsem.at[b]) for b in range(blocks)
    ]
    for copy in weights:
        copy.start()
    pl.semaphore_wait(barrier, 3 + neighbours)

    def hop(kind, t, block, target, own=False):
        first = t * chunk + (half if kind in (6, 8) else 0)
        where = pl.ds(first, half if kind in (5, 6, 7, 8) else chunk)
        return pltpu.make_async_remote_copy(
            src_ref=r.at[where] if own else rbuf.at[block, where],
            dst_ref=rbuf.at[block, where],
            send_sem=rsend.at[t, kind],
            recv_sem=rrecv.at[t, kind],
            device_id={"pb": target},
            device_id_type=MESH,
        )

    started = []

    def start(*what, **kw):
        copy = hop(*what, **kw)
        copy.start()
        started.append(copy)

    def send_own(t):
        start(1, t, p, across, own=True)
        start(2, t, p, along, own=True)
        start(0, t, p, core, own=True)

    def place(piece, source):
        if piece < CHUNKS:
            return qall.at[source, pl.ds(piece * chunk, chunk)]
        return pbuf.at[source]

    zsend_own, pass_on, finish = line(groups, z, place, zsend, zrecv)

    def multiply(t):
        rows = pl.ds(t * chunk, chunk)
        total = jnp.zeros((chunk, wbuf.shape[1]), jnp.float32)
        for b in range(blocks):
            total += lax.dot_general(
                rbuf[b, rows, :], wbuf[b], (((1,), (1,)), ((), ())), preferred_element_type=jnp.float32
            )
        grad = total.astype(jnp.bfloat16)
        product = grad.astype(jnp.float32) * outputs[rows, :].astype(jnp.float32)
        lane = lax.broadcasted_iota(jnp.int32, (chunk, LANES), 1)
        aux = base[rows, :]
        for h in range(heads):
            delta = -jnp.sum(product[:, h * width : (h + 1) * width], axis=1, keepdims=True)
            high = delta.astype(jnp.bfloat16).astype(jnp.float32)
            rest = delta - high
            middle = rest.astype(jnp.bfloat16).astype(jnp.float32)
            for i, part in enumerate((high, middle, rest - middle)):
                aux = jnp.where(lane == h * AUX + 3 + i, part, aux)
        grads[rows, :] = grad
        aux_rows[:, rows] = aux.T[: heads * AUX].astype(jnp.bfloat16)

    def rank():
        earlier = lax.broadcasted_iota(jnp.int32, (token_count, token_count), 0) < lax.broadcasted_iota(
            jnp.int32, (token_count, token_count), 1
        )
        earlier = earlier.astype(jnp.bfloat16)
        local = named.shape[0] // heads
        count = pbuf.shape[1] // heads
        for group in range(groups):
            marked = []
            for h in range(heads):
                ids = named[h * local : (h + 1) * local, :]
                hit = jnp.zeros((local, token_count), jnp.float32)
                for j in range(count):
                    at = h * count + j
                    hit += jnp.where(pbuf[group, at : at + 1, :] == ids, 1.0, 0.0)
                marked.append(hit)
            marked = jnp.concatenate(marked, axis=0)
            before = jnp.dot(marked.astype(jnp.bfloat16), earlier, preferred_element_type=jnp.float32)
            ranks = jnp.where(marked > 0.5, before, -1.0)
            rows_out[group] = ranks.astype(jnp.int32)
            padded = jnp.concatenate([ranks, jnp.zeros((LANES - ranks.shape[0], token_count), jnp.float32)], axis=0)
            cols_out[group] = padded.T.astype(jnp.int32)

    qall[z] = q[...]
    pbuf[z] = probes[...]
    send_own(0)
    for piece in (CHUNKS, *range(CHUNKS)):
        zsend_own(piece)
    send_own(1)
    own_block.wait()
    for t in range(CHUNKS + 1):
        if t < CHUNKS:
            hop(1, t, across, across).wait_recv()
            start(5, t, across, along)
            start(3, t, across, core)
            hop(2, t, along, along).wait_recv()
            start(6, t, along, across)
            start(4, t, along, core)
            if t + 2 < CHUNKS:
                send_own(t + 2)
        if 1 <= t <= CHUNKS:
            last = t - 1
            hop(5, last, corner, along).wait_recv()
            start(7, last, corner, core)
            hop(6, last, corner, across).wait_recv()
            start(8, last, corner, core)
        for piece, distance in PASSES.get(t, ()):
            pass_on(piece, distance)
        if 1 <= t <= CHUNKS:
            if t == 1:
                for copy in weights:
                    copy.wait()
            hop(0, last, core, core).wait_recv()
            hop(3, last, flip(2, core), core).wait_recv()
            hop(4, last, flip(4, core), core).wait_recv()
            hop(7, last, flip(1, corner), core).wait_recv()
            hop(8, last, flip(1, corner), core).wait_recv()
            multiply(last)
        if t == CHUNKS - 1:
            pass_on(CHUNKS, groups - 1)
            rank()

    for piece in range(CHUNKS):
        pass_on(piece, groups - 1)
    for copy in started:
        copy.wait_send()
    for piece in range(CHUNKS + 1):
        finish(piece)


def readout(readout_grad, readout_weight, outputs, base, queries, probes, named, groups, heads, width):
    token_count, depth = readout_grad.shape
    features = readout_weight.shape[0]
    blocks = lax.axis_size("pb")
    vmem = pl.BlockSpec(memory_space=pltpu.VMEM)
    pieces = CHUNKS + 1
    return pl.pallas_call(
        functools.partial(readout_kernel, groups, heads, width),
        in_specs=[vmem, pl.BlockSpec(memory_space=pl.ANY), vmem, vmem, vmem, vmem, vmem],
        out_specs=[vmem] * 5,
        out_shape=[
            jax.ShapeDtypeStruct((token_count, features), jnp.bfloat16),
            jax.ShapeDtypeStruct((heads * AUX, token_count), jnp.bfloat16),
            jax.ShapeDtypeStruct((groups, token_count, features), jnp.bfloat16),
            jax.ShapeDtypeStruct((groups, named.shape[0], token_count), jnp.int32),
            jax.ShapeDtypeStruct((groups, token_count, LANES), jnp.int32),
        ],
        scratch_shapes=[
            pltpu.VMEM((blocks, token_count, depth), jnp.bfloat16),
            pltpu.VMEM((blocks, features, depth), jnp.bfloat16),
            pltpu.VMEM((groups,) + probes.shape, jnp.int32),
            pltpu.SemaphoreType.DMA((CHUNKS, 9)),
            pltpu.SemaphoreType.DMA((CHUNKS, 9)),
            pltpu.SemaphoreType.DMA((pieces, groups, 2)),
            pltpu.SemaphoreType.DMA((pieces, groups)),
            pltpu.SemaphoreType.DMA,
            pltpu.SemaphoreType.DMA((blocks,)),
        ],
        compiler_params=pltpu.CompilerParams(
            collective_id=0, has_side_effects=True, vmem_limit_bytes=50 * 2**20
        ),
        cost_estimate=pl.CostEstimate(
            flops=2 * token_count * features * depth * blocks, bytes_accessed=32 * 2**20, transcendentals=0
        ),
    )(readout_grad, readout_weight, outputs, base, queries, probes, named)


def attend_kernel(
    groups, capacity, scale, counts, q, grads, aux_rows, rows, cols, keys, values, out,
    kbuf, vbuf, g, tbuf, aux, turned, partials, outgoing, arrived, ksem, vsem, ssem, rsem, zsend, zrecv
):
    me = lax.axis_index("grp")
    heads, local, span, width = kbuf.shape
    token_count = q.shape[1]
    contract_last = (((1,), (1,)), ((), ()))

    barrier = pltpu.get_barrier_semaphore()
    for d in range(1, groups):
        pl.semaphore_signal(
            barrier, inc=1, device_id={"grp": lax.rem(me + d, groups)}, device_id_type=MESH
        )

    def loads(h):
        return (
            pltpu.make_async_copy(keys.at[h], kbuf.at[h], ksem.at[h]),
            pltpu.make_async_copy(values.at[h], vbuf.at[h], vsem.at[h]),
        )

    def home(h, d):
        there = lax.rem(me + d, groups)
        return pltpu.make_async_remote_copy(
            src_ref=outgoing.at[h, there],
            dst_ref=arrived.at[h, d - 1],
            send_sem=ssem.at[h, d - 1],
            recv_sem=rsem.at[h, d - 1],
            device_id={"grp": there},
            device_id_type=MESH,
        )

    def spot_of(piece, source):
        if isinstance(piece, int) and piece == heads:
            return tbuf.at[source]
        return g.at[source, piece]

    send_own, pass_on, finish = line(groups, me, spot_of, zsend, zrecv)

    tbuf[me] = aux_rows[...]
    for h in range(heads):
        g[me, h] = grads[:, h * width : (h + 1) * width]
    pl.semaphore_wait(barrier, groups - 1)
    send_own(heads)
    send_own(0)
    send_own(1)
    for h in range(heads):
        for copy in loads(h):
            copy.start()
    pass_on(heads, 1)
    pass_on(0, 1)
    send_own(2)
    pass_on(heads, 2)
    pass_on(0, 2)
    send_own(3)
    pass_on(1, 1)
    pass_on(heads, groups - 1)
    for group in range(groups):
        wide = tbuf[group].astype(jnp.float32)
        wide = jnp.concatenate([wide, jnp.zeros((LANES - wide.shape[0], token_count), jnp.float32)], axis=0)
        aux[group] = wide.T.astype(jnp.bfloat16)
    later = [(1, 2), (2, 1), (2, 2), (3, 1), (3, 2)]

    lane = lax.broadcasted_iota(jnp.int32, (span, LANES), 1)
    key_id = lax.broadcasted_iota(jnp.int32, (span, LANES), 0)
    place = lax.broadcasted_iota(jnp.int32, (capacity, token_count), 0)
    spot = lax.broadcasted_iota(jnp.int32, (token_count, capacity), 1)

    def one_head(h, later):
        for copy in loads(h):
            copy.wait()
        pass_on(h, groups - 1)
        own = lane - h * AUX
        ones = jnp.where((own >= 0) & (own < 3), 1.0, 0.0)
        value_side = jnp.where((own >= 3) & (own < 6), 1.0, 0.0).astype(jnp.bfloat16)
        columns = pl.ds(pl.multiple_of(h * width, width), width)
        for c in range(local):
            valid = counts[h, c]
            key_side = jnp.where((lane == AUX - 1) & (key_id >= valid), -1e30, ones).astype(jnp.bfloat16)
            picked = []
            for group in range(groups):
                chosen = (rows[group, pl.ds(h * local + c, 1), :] == place).astype(jnp.bfloat16)
                rhs = jnp.concatenate(
                    [q[group, :, columns], aux[group], g[group, h]], axis=1
                )
                picked.append(jnp.dot(chosen, rhs, preferred_element_type=jnp.float32).astype(jnp.bfloat16))
            picked = jnp.concatenate(picked, axis=0)
            key_block, value_block = kbuf[h, c], vbuf[h, c]
            scores = lax.dot_general(
                picked[:, : 2 * LANES],
                jnp.concatenate([key_block, key_side], axis=1),
                contract_last,
                preferred_element_type=jnp.float32,
            )
            grad_prob = lax.dot_general(
                picked[:, LANES:],
                jnp.concatenate([value_side, value_block], axis=1),
                contract_last,
                preferred_element_type=jnp.float32,
            )
            grad_score = (jnp.exp(scores * scale) * grad_prob).astype(jnp.bfloat16)
            part = jnp.dot(grad_score, key_block, preferred_element_type=jnp.float32).astype(jnp.bfloat16)
            for group in range(groups):
                partials[group, c * capacity : (c + 1) * capacity, :] = part[
                    group * capacity : (group + 1) * capacity
                ]
            if c < len(later):
                pass_on(*later[c])
        for group in range(groups):
            turned[...] = pltpu.roll(cols[group], lax.rem(LANES - h * local, LANES), 1)
            chosen = jnp.concatenate(
                [(turned[:, c : c + 1] == spot).astype(jnp.bfloat16) for c in range(local)], axis=1
            )
            total = jnp.dot(chosen, partials[group], preferred_element_type=jnp.float32)
            outgoing[h, group] = (total * scale).astype(jnp.bfloat16)
        for d in range(1, groups):
            home(h, d).start()

    one_head(0, later)

    def next_head(h, carry):
        one_head(h, ())
        return carry

    lax.fori_loop(1, heads, next_head, 0)
    for h in range(heads):
        total = outgoing[h, me].astype(jnp.float32)
        for d in range(1, groups):
            home(h, d).wait_recv()
            total += arrived[h, d - 1].astype(jnp.float32)
        out[:, h * width : (h + 1) * width] = total.astype(out.dtype)
    for h in range(heads):
        for d in range(1, groups):
            home(h, d).wait_send()
    for piece in range(heads + 1):
        finish(piece)


def attend(counts, q, grads, aux_rows, rows, cols, keys, values, capacity, scale):
    groups, token_count, features = q.shape
    heads, local, span, width = keys.shape
    vmem = pl.BlockSpec(memory_space=pltpu.VMEM)
    hbm = pl.BlockSpec(memory_space=pl.ANY)
    return pl.pallas_call(
        functools.partial(attend_kernel, groups, capacity, scale),
        in_specs=[pl.BlockSpec(memory_space=pltpu.SMEM), vmem, vmem, vmem, vmem, vmem, hbm, hbm],
        out_specs=vmem,
        out_shape=jax.ShapeDtypeStruct((token_count, features), jnp.bfloat16),
        scratch_shapes=[
            pltpu.VMEM(keys.shape, jnp.bfloat16),
            pltpu.VMEM(values.shape, jnp.bfloat16),
            pltpu.VMEM((groups, heads, token_count, width), jnp.bfloat16),
            pltpu.VMEM((groups,) + aux_rows.shape, jnp.bfloat16),
            pltpu.VMEM((groups, token_count, LANES), jnp.bfloat16),
            pltpu.VMEM((token_count, LANES), jnp.int32),
            pltpu.VMEM((groups, local * capacity, width), jnp.bfloat16),
            pltpu.VMEM((heads, groups, token_count, width), jnp.bfloat16),
            pltpu.VMEM((heads, groups - 1, token_count, width), jnp.bfloat16),
            pltpu.SemaphoreType.DMA((heads,)),
            pltpu.SemaphoreType.DMA((heads,)),
            pltpu.SemaphoreType.DMA((heads, groups - 1)),
            pltpu.SemaphoreType.DMA((heads, groups - 1)),
            pltpu.SemaphoreType.DMA((heads + 1, groups, 2)),
            pltpu.SemaphoreType.DMA((heads + 1, groups)),
        ],
        compiler_params=pltpu.CompilerParams(
            collective_id=1, has_side_effects=True, vmem_limit_bytes=50 * 2**20
        ),
    )(counts, q, grads, aux_rows, rows, cols, keys, values)


def grad_kernel(groups, capacity, scale, counts, q, g, aux, rows, cols, keys, values, out, total):
    head, step = pl.program_id(0), pl.program_id(1)
    token_count = q.shape[0] // groups
    span = keys.shape[2]
    lane = lax.broadcasted_iota(jnp.int32, (span, LANES), 1)
    key_id = lax.broadcasted_iota(jnp.int32, (span, LANES), 0)
    own = lane - head * AUX
    ones = jnp.where((own >= 0) & (own < 3), 1.0, 0.0)
    value_side = jnp.where((own >= 3) & (own < 6), 1.0, 0.0).astype(jnp.bfloat16)
    place = lax.broadcasted_iota(jnp.int32, (capacity, token_count), 0)
    contract_last = (((1,), (1,)), ((), ()))
    partials = []
    for i in range(PAIR):
        valid = counts[head, step * PAIR + i]
        key_side = jnp.where((lane == AUX - 1) & (key_id >= valid), -1e30, ones).astype(jnp.bfloat16)
        key_block, value_block = keys[0, i], values[0, i]
        picked = []
        for group in range(groups):
            span_of = pl.ds(group * token_count, token_count)
            chosen = (rows[0, i, :, span_of] == place).astype(jnp.bfloat16)
            rhs = jnp.concatenate([q[span_of, :], aux[span_of, :], g[span_of, :]], axis=1)
            picked.append(jnp.dot(chosen, rhs, preferred_element_type=jnp.float32).astype(jnp.bfloat16))
        picked = jnp.concatenate(picked, axis=0)
        scores = lax.dot_general(
            picked[:, : 2 * LANES],
            jnp.concatenate([key_block, key_side], axis=1),
            contract_last,
            preferred_element_type=jnp.float32,
        )
        grad_prob = lax.dot_general(
            picked[:, LANES:],
            jnp.concatenate([value_side, value_block], axis=1),
            contract_last,
            preferred_element_type=jnp.float32,
        )
        grad_score = (jnp.exp(scores * scale) * grad_prob).astype(jnp.bfloat16)
        partials.append(jnp.dot(grad_score, key_block, preferred_element_type=jnp.float32).astype(jnp.bfloat16))
    spot = lax.broadcasted_iota(jnp.int32, (token_count, capacity), 1)
    for group in range(groups):
        span_of = pl.ds(group * token_count, token_count)
        chosen = jnp.concatenate(
            [(cols[0, 0, span_of, i : i + 1] == spot).astype(jnp.bfloat16) for i in range(PAIR)], axis=1
        )
        part = jnp.concatenate([p[group * capacity : (group + 1) * capacity] for p in partials], axis=0)
        add = jnp.dot(chosen, part, preferred_element_type=jnp.float32)

        @pl.when(step == 0)
        def _():
            total[span_of, :] = add

        @pl.when(step > 0)
        def _():
            total[span_of, :] += add

    @pl.when(step == pl.num_programs(1) - 1)
    def _():
        out[...] = (total[...] * scale).astype(out.dtype)


def shards(
    queries, outputs, readout_grad, readout_weight, log_norm, probes, owner_slots, counts, cluster_keys, values
):
    token_count = queries.shape[0]
    heads, local_clusters, span, width = cluster_keys.shape
    clusters = owner_slots.shape[1]
    groups = lax.axis_size("grp")
    capacity = 2 * token_count * probes.shape[2] // clusters
    scale = width ** (-0.5)
    every = groups * token_count

    steps = local_clusters // PAIR
    named = named_clusters(owner_slots, local_clusters)
    base = jnp.concatenate(
        [
            three_parts(log_norm * (-1.0 / scale)),
            jnp.zeros((token_count, heads, AUX - 4)),
            jnp.ones((token_count, heads, 1)),
        ],
        axis=2,
    ).reshape(token_count, heads * AUX)
    base = jnp.pad(base, ((0, 0), (0, LANES - heads * AUX)))

    if groups == 4 and heads == 4 and lax.axis_size("pb") == 8:
        grads, aux_rows, all_queries, rows, cols = readout(
            readout_grad,
            readout_weight,
            outputs,
            base,
            queries,
            probes.transpose(0, 2, 1).reshape(heads * probes.shape[2], token_count),
            named.reshape(heads * local_clusters, 1),
            groups,
            heads,
            width,
        )
        return attend(counts, all_queries, grads, aux_rows, rows, cols, cluster_keys, values, capacity, scale)

    probe_lanes = probes.transpose(1, 0, 2).reshape(token_count, heads * probes.shape[2])
    probe_lanes = jnp.pad(probe_lanes, ((0, 0), (0, LANES - probe_lanes.shape[1]))).astype(jnp.bfloat16)
    all_queries = lax.all_gather(jnp.concatenate([queries, probe_lanes], axis=1), "grp", axis=0, tiled=True)
    grad_out = lax.dot_general(
        lax.all_gather(readout_grad, "pb", axis=1, tiled=True),
        readout_weight,
        (((1,), (1,)), ((), ())),
        preferred_element_type=jnp.float32,
    ).astype(jnp.bfloat16)
    row_delta = jnp.sum(
        (grad_out.astype(jnp.float32) * outputs.astype(jnp.float32)).reshape(token_count, heads, width), axis=2
    )
    deltas = jnp.pad(three_parts(-row_delta), ((0, 0), (0, 0), (3, AUX - 6))).reshape(token_count, heads * AUX)
    aux = base + jnp.pad(deltas, ((0, 0), (0, LANES - heads * AUX)))
    all_grads = lax.all_gather(
        jnp.concatenate([grad_out, aux.astype(jnp.bfloat16)], axis=1), "grp", axis=0, tiled=True
    )

    all_probes = all_queries[:, heads * width : heads * width + heads * probes.shape[2]].astype(jnp.int32)
    all_probes = all_probes.reshape(every, heads, probes.shape[2]).transpose(1, 0, 2)
    ranks = probe_ranks(all_probes, named, token_count, groups)
    ranks = ranks.reshape(heads, local_clusters, 1, every)
    rank_cols = ranks.reshape(heads, steps, PAIR, every).transpose(0, 1, 3, 2)

    partial = pl.pallas_call(
        functools.partial(grad_kernel, groups, capacity, scale),
        grid=(heads, steps),
        in_specs=[
            pl.BlockSpec(memory_space=pltpu.SMEM),
            pl.BlockSpec((every, width), lambda h, c: (0, h)),
            pl.BlockSpec((every, width), lambda h, c: (0, h)),
            pl.BlockSpec((every, LANES), lambda h, c: (0, heads)),
            pl.BlockSpec((1, PAIR, 1, every), lambda h, c: (h, c, 0, 0)),
            pl.BlockSpec((1, 1, every, PAIR), lambda h, c: (h, c, 0, 0)),
            pl.BlockSpec((1, PAIR, span, width), lambda h, c: (h, c, 0, 0)),
            pl.BlockSpec((1, PAIR, span, width), lambda h, c: (h, c, 0, 0)),
        ],
        out_specs=pl.BlockSpec((every, width), lambda h, c: (0, h)),
        out_shape=jax.ShapeDtypeStruct((every, heads * width), jnp.bfloat16),
        scratch_shapes=[pltpu.VMEM((every, width), jnp.float32)],
        compiler_params=pltpu.CompilerParams(vmem_limit_bytes=50 * 2**20),
    )(counts, all_queries, all_grads, all_grads, ranks, rank_cols, cluster_keys, values)
    returned = lax.all_to_all(
        partial.reshape(groups, token_count, heads * width), "grp", split_axis=0, concat_axis=0, tiled=True
    )
    return jnp.sum(returned.astype(jnp.float32), axis=0).astype(jnp.bfloat16)


def solution(mesh):
    placed = (
        P("grp", "pb"),
        P("grp", "pb"),
        P("grp", "pb"),
        P("pb", None),
        P("grp", "pb"),
        P("pb", "grp", None),
        P("pb", None),
        P("pb", "grp"),
        P("pb", "grp", None, None),
        P("pb", "grp", None, None),
    )
    return jax.shard_map(shards, mesh=mesh, in_specs=placed, out_specs=P("grp", "pb"), check_vma=False)
```

```python
import functools

import jax
import jax.numpy as jnp
from jax import lax
from jax.experimental import pallas as pl
from jax.experimental.pallas import tpu as pltpu
from jax.sharding import PartitionSpec as P

LANES = 128
AUX = 8
PAIR = 2
CHUNKS = 4
EARLY = 2
MESH = pl.DeviceIdType.MESH
PASSES = {0: ((4, 1), (0, 1), (1, 1)), 1: ((2, 1), (3, 1), (4, 2), (0, 2)), 2: ((1, 2), (2, 2), (3, 2)), 3: ((5, 1),), 4: ((5, 2), (6, 1))}


def three_parts(x):
    high = lax.reduce_precision(x, 8, 7)
    rest = x - high
    middle = lax.reduce_precision(rest, 8, 7)
    return jnp.stack([high, middle, rest - middle], axis=-1)


def named_clusters(owner_slots, local_clusters):
    cluster_ids = jnp.arange(owner_slots.shape[1], dtype=jnp.int32)
    slots = lax.axis_index("grp") * local_clusters + jnp.arange(local_clusters, dtype=jnp.int32)
    return jnp.sum(jnp.where(owner_slots[:, None, :] == slots[None, :, None], cluster_ids, 0), axis=2, dtype=jnp.int32)


def probe_ranks(probes, named, token_count, groups):
    local_clusters = named.shape[1]
    marked = jnp.any(probes[:, None, :, :] == named[:, :, None, None], axis=3)
    marked = marked.reshape(probes.shape[0], local_clusters, groups, token_count)
    earlier = jnp.arange(token_count)[:, None] < jnp.arange(token_count)[None, :]
    before = lax.dot_general(
        marked.astype(jnp.bfloat16),
        earlier.astype(jnp.bfloat16),
        (((3,), (0,)), ((), ())),
        preferred_element_type=jnp.float32,
    )
    return jnp.where(marked, before.astype(jnp.int32), -1)


def line(groups, z, place, zsend, zrecv):
    def hop(piece, source, way):
        where = place(piece, source)
        return pltpu.make_async_remote_copy(
            src_ref=where,
            dst_ref=where,
            send_sem=zsend.at[piece, source, (way + 1) // 2],
            recv_sem=zrecv.at[piece, source],
            device_id={"grp": z + way},
            device_id_type=MESH,
        )

    def inside(q):
        return (q >= 0) & (q < groups)

    def send_own(piece):
        for way in (1, -1):

            @pl.when(inside(z + way))
            def _():
                hop(piece, z, way).start()

    def pass_on(piece, distance):
        for way in (1, -1):
            source = z - way * distance

            @pl.when(inside(source))
            def _():
                hop(piece, source, way).wait_recv()

            @pl.when(inside(source) & inside(z + way))
            def _():
                hop(piece, source, way).start()

    def finish(piece):
        for distance in range(groups - 1):
            for way in (1, -1):
                source = z - way * distance

                @pl.when(inside(source) & inside(z + way))
                def _():
                    hop(piece, source, way).wait_send()

    return send_own, pass_on, finish


def readout_kernel(
    groups, heads, width, r, w, outputs, base, q, probes, named, grads, first, aux_rows, qall, rows_out, cols_out, rbuf, wbuf, pbuf,
    rsend, rrecv, zsend, zrecv, local_sem, wsem
):
    p, z = lax.axis_index("pb"), lax.axis_index("grp")
    token_count, depth = r.shape
    blocks = rbuf.shape[0]
    chunk = token_count // CHUNKS
    half = chunk // 2

    def flip(bit, q):
        return q + bit - 2 * bit * lax.rem(lax.div(q, bit), 2)

    core, across, along = flip(1, p), flip(2, p), flip(4, p)
    corner = flip(4, across)
    has_left, has_right = z > 0, z < groups - 1
    neighbours = jnp.where(has_left, 1, 0) + jnp.where(has_right, 1, 0)

    barrier = pltpu.get_barrier_semaphore()
    for other in (core, across, along):
        pl.semaphore_signal(barrier, inc=1, device_id={"pb": other}, device_id_type=MESH)

    @pl.when(has_left)
    def _():
        pl.semaphore_signal(barrier, inc=1, device_id={"grp": z - 1}, device_id_type=MESH)

    @pl.when(has_right)
    def _():
        pl.semaphore_signal(barrier, inc=1, device_id={"grp": z + 1}, device_id_type=MESH)

    own_block = pltpu.make_async_copy(r, rbuf.at[p], local_sem)
    own_block.start()
    weights = [
        pltpu.make_async_copy(w.at[:, pl.ds(b * depth, depth)], wbuf.at[b], wsem.at[b]) for b in range(blocks)
    ]
    for copy in weights:
        copy.start()
    pl.semaphore_wait(barrier, 3 + neighbours)

    def hop(kind, t, block, target, own=False):
        first = t * chunk + (half if kind in (6, 8) else 0)
        where = pl.ds(first, half if kind in (5, 6, 7, 8) else chunk)
        return pltpu.make_async_remote_copy(
            src_ref=r.at[where] if own else rbuf.at[block, where],
            dst_ref=rbuf.at[block, where],
            send_sem=rsend.at[t, kind],
            recv_sem=rrecv.at[t, kind],
            device_id={"pb": target},
            device_id_type=MESH,
        )

    started = []

    def start(*what, **kw):
        copy = hop(*what, **kw)
        copy.start()
        started.append(copy)

    def send_own(t):
        start(1, t, p, across, own=True)
        start(2, t, p, along, own=True)
        start(0, t, p, core, own=True)

    def place(piece, source):
        if piece < CHUNKS:
            return qall.at[source, pl.ds(piece * chunk, chunk)]
        if piece == CHUNKS:
            return pbuf.at[source]
        return first.at[source, pl.ds((piece - CHUNKS - 1) * chunk, chunk)]

    zsend_own, pass_on, finish = line(groups, z, place, zsend, zrecv)

    def multiply(t):
        rows = pl.ds(t * chunk, chunk)
        total = jnp.zeros((chunk, wbuf.shape[1]), jnp.float32)
        for b in range(blocks):
            total += lax.dot_general(
                rbuf[b, rows, :], wbuf[b], (((1,), (1,)), ((), ())), preferred_element_type=jnp.float32
            )
        grad = total.astype(jnp.bfloat16)
        product = grad.astype(jnp.float32) * outputs[rows, :].astype(jnp.float32)
        lane = lax.broadcasted_iota(jnp.int32, (chunk, LANES), 1)
        aux = base[rows, :]
        for h in range(heads):
            delta = -jnp.sum(product[:, h * width : (h + 1) * width], axis=1, keepdims=True)
            high = delta.astype(jnp.bfloat16).astype(jnp.float32)
            rest = delta - high
            middle = rest.astype(jnp.bfloat16).astype(jnp.float32)
            for i, part in enumerate((high, middle, rest - middle)):
                aux = jnp.where(lane == h * AUX + 3 + i, part, aux)
        if t < EARLY:
            first[z, rows, :] = grad
        else:
            grads[pl.ds((t - EARLY) * chunk, chunk), :] = grad
        aux_rows[:, rows] = aux.T[: heads * AUX].astype(jnp.bfloat16)

    def rank():
        earlier = lax.broadcasted_iota(jnp.int32, (token_count, token_count), 0) < lax.broadcasted_iota(
            jnp.int32, (token_count, token_count), 1
        )
        earlier = earlier.astype(jnp.bfloat16)
        local = named.shape[0] // heads
        count = pbuf.shape[1] // heads
        for group in range(groups):
            marked = []
            for h in range(heads):
                ids = named[h * local : (h + 1) * local, :]
                hit = jnp.zeros((local, token_count), jnp.float32)
                for j in range(count):
                    at = h * count + j
                    hit += jnp.where(pbuf[group, at : at + 1, :] == ids, 1.0, 0.0)
                marked.append(hit)
            marked = jnp.concatenate(marked, axis=0)
            before = jnp.dot(marked.astype(jnp.bfloat16), earlier, preferred_element_type=jnp.float32)
            ranks = jnp.where(marked > 0.5, before, -1.0)
            rows_out[group] = ranks.astype(jnp.int32)
            padded = jnp.concatenate([ranks, jnp.zeros((LANES - ranks.shape[0], token_count), jnp.float32)], axis=0)
            cols_out[group] = padded.T.astype(jnp.int32)

    qall[z] = q[...]
    pbuf[z] = probes[...]
    send_own(0)
    for piece in (CHUNKS, *range(CHUNKS)):
        zsend_own(piece)
    send_own(1)
    own_block.wait()
    for t in range(CHUNKS + 1):
        if t < CHUNKS:
            hop(1, t, across, across).wait_recv()
            start(5, t, across, along)
            start(3, t, across, core)
            hop(2, t, along, along).wait_recv()
            start(6, t, along, across)
            start(4, t, along, core)
            if t + 2 < CHUNKS:
                send_own(t + 2)
        if 1 <= t <= CHUNKS:
            last = t - 1
            hop(5, last, corner, along).wait_recv()
            start(7, last, corner, core)
            hop(6, last, corner, across).wait_recv()
            start(8, last, corner, core)
        for piece, distance in PASSES.get(t, ()):
            pass_on(piece, distance)
        if 1 <= t <= CHUNKS:
            if t == 1:
                for copy in weights:
                    copy.wait()
            hop(0, last, core, core).wait_recv()
            hop(3, last, flip(2, core), core).wait_recv()
            hop(4, last, flip(4, core), core).wait_recv()
            hop(7, last, flip(1, corner), core).wait_recv()
            hop(8, last, flip(1, corner), core).wait_recv()
            multiply(last)
            if last < EARLY:
                zsend_own(CHUNKS + 1 + last)
        if t == CHUNKS - 1:
            pass_on(CHUNKS, groups - 1)
            rank()

    pass_on(CHUNKS + EARLY, 2)
    for piece in (*range(CHUNKS), *range(CHUNKS + 1, CHUNKS + 1 + EARLY)):
        pass_on(piece, groups - 1)
    for copy in started:
        copy.wait_send()
    for piece in range(CHUNKS + 1 + EARLY):
        finish(piece)


def readout(readout_grad, readout_weight, outputs, base, queries, probes, named, groups, heads, width):
    token_count, depth = readout_grad.shape
    features = readout_weight.shape[0]
    blocks = lax.axis_size("pb")
    vmem = pl.BlockSpec(memory_space=pltpu.VMEM)
    pieces = CHUNKS + 1 + EARLY
    early = token_count // CHUNKS * EARLY
    return pl.pallas_call(
        functools.partial(readout_kernel, groups, heads, width),
        in_specs=[vmem, pl.BlockSpec(memory_space=pl.ANY), vmem, vmem, vmem, vmem, vmem],
        out_specs=[vmem] * 6,
        out_shape=[
            jax.ShapeDtypeStruct((token_count - early, features), jnp.bfloat16),
            jax.ShapeDtypeStruct((groups, early, features), jnp.bfloat16),
            jax.ShapeDtypeStruct((heads * AUX, token_count), jnp.bfloat16),
            jax.ShapeDtypeStruct((groups, token_count, features), jnp.bfloat16),
            jax.ShapeDtypeStruct((groups, named.shape[0], token_count), jnp.int32),
            jax.ShapeDtypeStruct((groups, token_count, LANES), jnp.int32),
        ],
        scratch_shapes=[
            pltpu.VMEM((blocks, token_count, depth), jnp.bfloat16),
            pltpu.VMEM((blocks, features, depth), jnp.bfloat16),
            pltpu.VMEM((groups,) + probes.shape, jnp.int32),
            pltpu.SemaphoreType.DMA((CHUNKS, 9)),
            pltpu.SemaphoreType.DMA((CHUNKS, 9)),
            pltpu.SemaphoreType.DMA((pieces, groups, 2)),
            pltpu.SemaphoreType.DMA((pieces, groups)),
            pltpu.SemaphoreType.DMA,
            pltpu.SemaphoreType.DMA((blocks,)),
        ],
        compiler_params=pltpu.CompilerParams(
            collective_id=0, has_side_effects=True, vmem_limit_bytes=50 * 2**20
        ),
        cost_estimate=pl.CostEstimate(
            flops=2 * token_count * features * depth * blocks, bytes_accessed=32 * 2**20, transcendentals=0
        ),
    )(readout_grad, readout_weight, outputs, base, queries, probes, named)


def attend_kernel(
    groups, capacity, scale, counts, q, grads, first, aux_rows, rows, cols, keys, values, out,
    kbuf, vbuf, g, tbuf, aux, turned, partials, outgoing, arrived, ksem, vsem, ssem, rsem, zsend, zrecv
):
    me = lax.axis_index("grp")
    heads, local, span, width = kbuf.shape
    token_count = q.shape[1]
    contract_last = (((1,), (1,)), ((), ()))

    barrier = pltpu.get_barrier_semaphore()
    for d in range(1, groups):
        pl.semaphore_signal(
            barrier, inc=1, device_id={"grp": lax.rem(me + d, groups)}, device_id_type=MESH
        )

    def loads(h):
        return (
            pltpu.make_async_copy(keys.at[h], kbuf.at[h], ksem.at[h]),
            pltpu.make_async_copy(values.at[h], vbuf.at[h], vsem.at[h]),
        )

    def home(h, d):
        there = lax.rem(me + d, groups)
        return pltpu.make_async_remote_copy(
            src_ref=outgoing.at[h, there],
            dst_ref=arrived.at[h, d - 1],
            send_sem=ssem.at[h, d - 1],
            recv_sem=rsem.at[h, d - 1],
            device_id={"grp": there},
            device_id_type=MESH,
        )

    def spot_of(piece, source):
        if isinstance(piece, int) and piece == heads:
            return tbuf.at[source]
        return g.at[source, piece, pl.ds(early, token_count - early)]

    early = first.shape[1]
    send_own, pass_on, finish = line(groups, me, spot_of, zsend, zrecv)

    tbuf[me] = aux_rows[...]
    for h in range(heads):
        g[me, h, early:, :] = grads[:, h * width : (h + 1) * width]
    pl.semaphore_wait(barrier, groups - 1)
    send_own(heads)
    send_own(0)
    send_own(1)
    for h in range(heads):
        for copy in loads(h):
            copy.start()
    for group in range(groups):
        for h in range(heads):
            g[group, h, :early, :] = first[group, :, h * width : (h + 1) * width]
    pass_on(heads, 1)
    pass_on(0, 1)
    send_own(2)
    pass_on(heads, 2)
    pass_on(0, 2)
    send_own(3)
    pass_on(1, 1)
    pass_on(heads, groups - 1)
    for group in range(groups):
        wide = tbuf[group].astype(jnp.float32)
        wide = jnp.concatenate([wide, jnp.zeros((LANES - wide.shape[0], token_count), jnp.float32)], axis=0)
        aux[group] = wide.T.astype(jnp.bfloat16)
    later = [(1, 2), (2, 1), (2, 2), (3, 1), (3, 2)]

    lane = lax.broadcasted_iota(jnp.int32, (span, LANES), 1)
    key_id = lax.broadcasted_iota(jnp.int32, (span, LANES), 0)
    place = lax.broadcasted_iota(jnp.int32, (capacity, token_count), 0)
    spot = lax.broadcasted_iota(jnp.int32, (token_count, capacity), 1)

    def one_head(h, later):
        for copy in loads(h):
            copy.wait()
        pass_on(h, groups - 1)
        own = lane - h * AUX
        ones = jnp.where((own >= 0) & (own < 3), 1.0, 0.0)
        value_side = jnp.where((own >= 3) & (own < 6), 1.0, 0.0).astype(jnp.bfloat16)
        columns = pl.ds(pl.multiple_of(h * width, width), width)
        for c in range(local):
            valid = counts[h, c]
            key_side = jnp.where((lane == AUX - 1) & (key_id >= valid), -1e30, ones).astype(jnp.bfloat16)
            picked = []
            for group in range(groups):
                chosen = (rows[group, pl.ds(h * local + c, 1), :] == place).astype(jnp.bfloat16)
                rhs = jnp.concatenate(
                    [q[group, :, columns], aux[group], g[group, h]], axis=1
                )
                picked.append(jnp.dot(chosen, rhs, preferred_element_type=jnp.float32).astype(jnp.bfloat16))
            picked = jnp.concatenate(picked, axis=0)
            key_block, value_block = kbuf[h, c], vbuf[h, c]
            scores = lax.dot_general(
                picked[:, : 2 * LANES],
                jnp.concatenate([key_block, key_side], axis=1),
                contract_last,
                preferred_element_type=jnp.float32,
            )
            grad_prob = lax.dot_general(
                picked[:, LANES:],
                jnp.concatenate([value_side, value_block], axis=1),
                contract_last,
                preferred_element_type=jnp.float32,
            )
            grad_score = (jnp.exp(scores * scale) * grad_prob).astype(jnp.bfloat16)
            part = jnp.dot(grad_score, key_block, preferred_element_type=jnp.float32).astype(jnp.bfloat16)
            for group in range(groups):
                partials[group, c * capacity : (c + 1) * capacity, :] = part[
                    group * capacity : (group + 1) * capacity
                ]
            if c < len(later):
                pass_on(*later[c])
        for group in range(groups):
            turned[...] = pltpu.roll(cols[group], lax.rem(LANES - h * local, LANES), 1)
            chosen = jnp.concatenate(
                [(turned[:, c : c + 1] == spot).astype(jnp.bfloat16) for c in range(local)], axis=1
            )
            total = jnp.dot(chosen, partials[group], preferred_element_type=jnp.float32)
            outgoing[h, group] = (total * scale).astype(jnp.bfloat16)
        for d in range(1, groups):
            home(h, d).start()

    one_head(0, later)

    def next_head(h, carry):
        one_head(h, ())
        return carry

    lax.fori_loop(1, heads, next_head, 0)
    for h in range(heads):
        total = outgoing[h, me].astype(jnp.float32)
        for d in range(1, groups):
            home(h, d).wait_recv()
            total += arrived[h, d - 1].astype(jnp.float32)
        out[:, h * width : (h + 1) * width] = total.astype(out.dtype)
    for h in range(heads):
        for d in range(1, groups):
            home(h, d).wait_send()
    for piece in range(heads + 1):
        finish(piece)


def attend(counts, q, grads, first, aux_rows, rows, cols, keys, values, capacity, scale):
    groups, token_count, features = q.shape
    heads, local, span, width = keys.shape
    vmem = pl.BlockSpec(memory_space=pltpu.VMEM)
    hbm = pl.BlockSpec(memory_space=pl.ANY)
    return pl.pallas_call(
        functools.partial(attend_kernel, groups, capacity, scale),
        in_specs=[pl.BlockSpec(memory_space=pltpu.SMEM), vmem, vmem, vmem, vmem, vmem, vmem, hbm, hbm],
        out_specs=vmem,
        out_shape=jax.ShapeDtypeStruct((token_count, features), jnp.bfloat16),
        scratch_shapes=[
            pltpu.VMEM(keys.shape, jnp.bfloat16),
            pltpu.VMEM(values.shape, jnp.bfloat16),
            pltpu.VMEM((groups, heads, token_count, width), jnp.bfloat16),
            pltpu.VMEM((groups,) + aux_rows.shape, jnp.bfloat16),
            pltpu.VMEM((groups, token_count, LANES), jnp.bfloat16),
            pltpu.VMEM((token_count, LANES), jnp.int32),
            pltpu.VMEM((groups, local * capacity, width), jnp.bfloat16),
            pltpu.VMEM((heads, groups, token_count, width), jnp.bfloat16),
            pltpu.VMEM((heads, groups - 1, token_count, width), jnp.bfloat16),
            pltpu.SemaphoreType.DMA((heads,)),
            pltpu.SemaphoreType.DMA((heads,)),
            pltpu.SemaphoreType.DMA((heads, groups - 1)),
            pltpu.SemaphoreType.DMA((heads, groups - 1)),
            pltpu.SemaphoreType.DMA((heads + 1, groups, 2)),
            pltpu.SemaphoreType.DMA((heads + 1, groups)),
        ],
        compiler_params=pltpu.CompilerParams(
            collective_id=1, has_side_effects=True, vmem_limit_bytes=50 * 2**20
        ),
    )(counts, q, grads, first, aux_rows, rows, cols, keys, values)


def grad_kernel(groups, capacity, scale, counts, q, g, aux, rows, cols, keys, values, out, total):
    head, step = pl.program_id(0), pl.program_id(1)
    token_count = q.shape[0] // groups
    span = keys.shape[2]
    lane = lax.broadcasted_iota(jnp.int32, (span, LANES), 1)
    key_id = lax.broadcasted_iota(jnp.int32, (span, LANES), 0)
    own = lane - head * AUX
    ones = jnp.where((own >= 0) & (own < 3), 1.0, 0.0)
    value_side = jnp.where((own >= 3) & (own < 6), 1.0, 0.0).astype(jnp.bfloat16)
    place = lax.broadcasted_iota(jnp.int32, (capacity, token_count), 0)
    contract_last = (((1,), (1,)), ((), ()))
    partials = []
    for i in range(PAIR):
        valid = counts[head, step * PAIR + i]
        key_side = jnp.where((lane == AUX - 1) & (key_id >= valid), -1e30, ones).astype(jnp.bfloat16)
        key_block, value_block = keys[0, i], values[0, i]
        picked = []
        for group in range(groups):
            span_of = pl.ds(group * token_count, token_count)
            chosen = (rows[0, i, :, span_of] == place).astype(jnp.bfloat16)
            rhs = jnp.concatenate([q[span_of, :], aux[span_of, :], g[span_of, :]], axis=1)
            picked.append(jnp.dot(chosen, rhs, preferred_element_type=jnp.float32).astype(jnp.bfloat16))
        picked = jnp.concatenate(picked, axis=0)
        scores = lax.dot_general(
            picked[:, : 2 * LANES],
            jnp.concatenate([key_block, key_side], axis=1),
            contract_last,
            preferred_element_type=jnp.float32,
        )
        grad_prob = lax.dot_general(
            picked[:, LANES:],
            jnp.concatenate([value_side, value_block], axis=1),
            contract_last,
            preferred_element_type=jnp.float32,
        )
        grad_score = (jnp.exp(scores * scale) * grad_prob).astype(jnp.bfloat16)
        partials.append(jnp.dot(grad_score, key_block, preferred_element_type=jnp.float32).astype(jnp.bfloat16))
    spot = lax.broadcasted_iota(jnp.int32, (token_count, capacity), 1)
    for group in range(groups):
        span_of = pl.ds(group * token_count, token_count)
        chosen = jnp.concatenate(
            [(cols[0, 0, span_of, i : i + 1] == spot).astype(jnp.bfloat16) for i in range(PAIR)], axis=1
        )
        part = jnp.concatenate([p[group * capacity : (group + 1) * capacity] for p in partials], axis=0)
        add = jnp.dot(chosen, part, preferred_element_type=jnp.float32)

        @pl.when(step == 0)
        def _():
            total[span_of, :] = add

        @pl.when(step > 0)
        def _():
            total[span_of, :] += add

    @pl.when(step == pl.num_programs(1) - 1)
    def _():
        out[...] = (total[...] * scale).astype(out.dtype)


def shards(
    queries, outputs, readout_grad, readout_weight, log_norm, probes, owner_slots, counts, cluster_keys, values
):
    token_count = queries.shape[0]
    heads, local_clusters, span, width = cluster_keys.shape
    clusters = owner_slots.shape[1]
    groups = lax.axis_size("grp")
    capacity = 2 * token_count * probes.shape[2] // clusters
    scale = width ** (-0.5)
    every = groups * token_count

    steps = local_clusters // PAIR
    named = named_clusters(owner_slots, local_clusters)
    base = jnp.concatenate(
        [
            three_parts(log_norm * (-1.0 / scale)),
            jnp.zeros((token_count, heads, AUX - 4)),
            jnp.ones((token_count, heads, 1)),
        ],
        axis=2,
    ).reshape(token_count, heads * AUX)
    base = jnp.pad(base, ((0, 0), (0, LANES - heads * AUX)))

    if groups == 4 and heads == 4 and lax.axis_size("pb") == 8:
        grads, first, aux_rows, all_queries, rows, cols = readout(
            readout_grad,
            readout_weight,
            outputs,
            base,
            queries,
            probes.transpose(0, 2, 1).reshape(heads * probes.shape[2], token_count),
            named.reshape(heads * local_clusters, 1),
            groups,
            heads,
            width,
        )
        return attend(counts, all_queries, grads, first, aux_rows, rows, cols, cluster_keys, values, capacity, scale)

    probe_lanes = probes.transpose(1, 0, 2).reshape(token_count, heads * probes.shape[2])
    probe_lanes = jnp.pad(probe_lanes, ((0, 0), (0, LANES - probe_lanes.shape[1]))).astype(jnp.bfloat16)
    all_queries = lax.all_gather(jnp.concatenate([queries, probe_lanes], axis=1), "grp", axis=0, tiled=True)
    grad_out = lax.dot_general(
        lax.all_gather(readout_grad, "pb", axis=1, tiled=True),
        readout_weight,
        (((1,), (1,)), ((), ())),
        preferred_element_type=jnp.float32,
    ).astype(jnp.bfloat16)
    row_delta = jnp.sum(
        (grad_out.astype(jnp.float32) * outputs.astype(jnp.float32)).reshape(token_count, heads, width), axis=2
    )
    deltas = jnp.pad(three_parts(-row_delta), ((0, 0), (0, 0), (3, AUX - 6))).reshape(token_count, heads * AUX)
    aux = base + jnp.pad(deltas, ((0, 0), (0, LANES - heads * AUX)))
    all_grads = lax.all_gather(
        jnp.concatenate([grad_out, aux.astype(jnp.bfloat16)], axis=1), "grp", axis=0, tiled=True
    )

    all_probes = all_queries[:, heads * width : heads * width + heads * probes.shape[2]].astype(jnp.int32)
    all_probes = all_probes.reshape(every, heads, probes.shape[2]).transpose(1, 0, 2)
    ranks = probe_ranks(all_probes, named, token_count, groups)
    ranks = ranks.reshape(heads, local_clusters, 1, every)
    rank_cols = ranks.reshape(heads, steps, PAIR, every).transpose(0, 1, 3, 2)

    partial = pl.pallas_call(
        functools.partial(grad_kernel, groups, capacity, scale),
        grid=(heads, steps),
        in_specs=[
            pl.BlockSpec(memory_space=pltpu.SMEM),
            pl.BlockSpec((every, width), lambda h, c: (0, h)),
            pl.BlockSpec((every, width), lambda h, c: (0, h)),
            pl.BlockSpec((every, LANES), lambda h, c: (0, heads)),
            pl.BlockSpec((1, PAIR, 1, every), lambda h, c: (h, c, 0, 0)),
            pl.BlockSpec((1, 1, every, PAIR), lambda h, c: (h, c, 0, 0)),
            pl.BlockSpec((1, PAIR, span, width), lambda h, c: (h, c, 0, 0)),
            pl.BlockSpec((1, PAIR, span, width), lambda h, c: (h, c, 0, 0)),
        ],
        out_specs=pl.BlockSpec((every, width), lambda h, c: (0, h)),
        out_shape=jax.ShapeDtypeStruct((every, heads * width), jnp.bfloat16),
        scratch_shapes=[pltpu.VMEM((every, width), jnp.float32)],
        compiler_params=pltpu.CompilerParams(vmem_limit_bytes=50 * 2**20),
    )(counts, all_queries, all_grads, all_grads, ranks, rank_cols, cluster_keys, values)
    returned = lax.all_to_all(
        partial.reshape(groups, token_count, heads * width), "grp", split_axis=0, concat_axis=0, tiled=True
    )
    return jnp.sum(returned.astype(jnp.float32), axis=0).astype(jnp.bfloat16)


def solution(mesh):
    placed = (
        P("grp", "pb"),
        P("grp", "pb"),
        P("grp", "pb"),
        P("pb", None),
        P("grp", "pb"),
        P("pb", "grp", None),
        P("pb", None),
        P("pb", "grp"),
        P("pb", "grp", None, None),
        P("pb", "grp", None, None),
    )
    return jax.shard_map(shards, mesh=mesh, in_specs=placed, out_specs=P("grp", "pb"), check_vma=False)
```
